128 devices in a mesh: dp: 8 (over z, x_lo), expert: 16 (over y, x_hi, core).
Axes of the slice: x: 4 (x_hi: 2, x_lo: 2; x = x_hi * 2 + x_lo), y: 4, z: 4, core: 2. Of those that a mesh axis runs over, the one named last changes fastest.
Arguments:
- tokens: bfloat16 [768, 7168], P('expert', 'dp'), may hold values from -6 to 6
- upstream: bfloat16 [768, 7168], P('expert', 'dp'), may hold values from -6 to 6
- expert_ids: int32 [768, 4], P('expert'), may hold values from 0 to 31, all different within a row; in each aligned block of 48 rows (0 to 47, 48 to 95, ...) at most 8 rows name the same one
- gate_values: float32 [768, 4], P('expert'), may hold values from 0.2 to 1
- gate_weight: bfloat16 [32, 7168, 1024], P('expert', None, 'dp'), may hold values from -0.0625 to 0.0625
- up_weight: bfloat16 [32, 7168, 1024], P('expert', None, 'dp'), may hold values from -0.0625 to 0.0625
- down_weight: bfloat16 [32, 1024, 7168], P('expert', 'dp'), may hold values from -0.1875 to 0.1875
Outputs:
- mixed: bfloat16 [768, 7168], P('expert', 'dp')
- token_grads: bfloat16 [768, 7168], P('expert', 'dp')
- gate_weight_grad: bfloat16 [32, 7168, 1024], P('expert', None, 'dp')
- up_weight_grad: bfloat16 [32, 7168, 1024], P('expert', None, 'dp')
- down_weight_grad: bfloat16 [32, 1024, 7168], P('expert', 'dp')
The draws below stay inside these ranges and needn't reach their ends.
Inputs may be any that keep to these rules, and one draw needn't show every extreme that they name: `expert_ids`: each row names 4 different experts; among the rows of one device's block of 48 tokens no expert is named more than 8 times, a bound that some block reaches.
All inputs are finite; a program needn't handle non-finite values.
Results may differ from the reference program's by a relative error of at most 0.02.
Values may be sent and summed in bfloat16 or wider, within the bound.
No kernel may reach another device: no remote copies, remote signals or barrier semaphores. Data moves between devices by JAX's collectives and lax.ppermute only.
A program may use at most 320 MiB of HBM per device.

```python
import math
import jax
import jax.numpy as jnp
import numpy as np
from jax import lax

D = 7168
HID_DEV = 128
EXP_DEV = 2
TOPK = 4
TOK_DEV = 48
FF = 1024
EXPERTS = 32
CAP = 8
TOKENS = 768
N_DP = 8
N_EXPERT = 16


def shard_levels(stream_key, extent, pieces, smallest, largest):
    level = 1.0
    for dim, parts in pieces:
        steps = jax.random.uniform(jax.random.fold_in(jax.random.fold_in(stream_key, 6), dim), (parts,), jnp.float32, smallest / len(pieces), largest / len(pieces))
        level = level * jnp.repeat(jnp.exp(steps), extent[dim] // parts).reshape((-1,) + (1,) * (len(extent) - 1 - dim))
    return level


def deal_out(stream_key, own, number, rows, number_of, top, limit, skew):
    order = jax.random.permutation(stream_key, number_of)
    heavy_load, usual = load_shares(number_of, rows * top, limit, skew, True), load_shares(number_of, rows * top, limit, skew, False)
    places = jnp.arange(number_of)

    def named(sizes, rotation):
        used = int((sizes > 0).sum())
        fixed = max(1, used // 4)
        shifted = fixed + (places - fixed + rotation * (used - fixed)) % max(1, number_of - fixed)
        return jnp.zeros((number_of,), jnp.int32).at[order[jnp.where(places < fixed, places, shifted)]].set(jnp.asarray(sizes, jnp.int32))

    sizes = jnp.where(number % 4 == 0, named(heavy_load, number // 4), named(usual, number - number // 4 - 1))
    mixed = jax.random.permutation(jax.random.fold_in(own, 3), number_of)
    giver, taker = mixed[0:number_of // 2 * 2:2], mixed[1:number_of // 2 * 2:2]
    slack = jnp.minimum(sizes[giver] - 1, limit - sizes[taker]) // 2
    slack = jnp.where((giver == order[0]) | (taker == order[0]) | (sizes[taker] == 0), 0, jnp.maximum(slack, 0))
    shifted = jax.random.randint(jax.random.fold_in(own, 4), (number_of // 2,), 0, 1 << 20) % (slack + 1)
    sizes = sizes.at[giver].add(-shifted).at[taker].add(shifted)
    items = jnp.searchsorted(jnp.cumsum(sizes), jnp.arange(rows * top), side="right").astype(jnp.int32)
    table = items.reshape(top, rows).T
    table = table[jax.random.permutation(jax.random.fold_in(own, 1), rows)]
    rotation = jax.random.randint(jax.random.fold_in(own, 2), (rows, 1), 0, top)
    return jnp.take_along_axis(table, (jnp.arange(top)[None, :] + rotation) % top, axis=1)


def load_shares(number_of, total, limit, lean, full):
    portions = [(1 << 20) // math.isqrt(rank ** lean) + 1 for rank in range(1, number_of + 1)]
    largest = limit if full else min(limit, max(-(-total // number_of), total * portions[0] // sum(portions)))
    least = 1 if total - largest >= number_of - 1 else 0
    counts, surplus = [largest] + [least] * (number_of - 1), total - largest - least * (number_of - 1)
    while surplus > 0:
        movable = [i for i in range(1, number_of) if counts[i] < largest] or [i for i in range(1, number_of) if counts[i] < limit]
        pool, budget = sum([portions[i] for i in movable]), surplus
        for i in movable:
            extra = min(limit - counts[i], max(1, budget * portions[i] // pool), surplus)
            counts[i] = counts[i] + extra
            surplus = surplus - extra
    return np.array(counts)


def bell_draw(key, shape, scale, limit, shards=(), held_as=jnp.bfloat16):
    values = scale * jax.random.normal(key, shape, jnp.float32)
    if shards:
        values = values * shard_levels(key, shape, shards, -0.22, 0.18)
    return jnp.clip(values, -limit, limit).astype(held_as)


def setup_inputs(seed: int = 0) -> dict:
    seeds = jax.random.split(jax.random.key(seed), 8)
    tokens = bell_draw(seeds[0], (TOKENS, D), 1.0, 6.0, ((0, 16), (1, 8)))
    upstream = bell_draw(seeds[1], (TOKENS, D), 1.0, 6.0, ((0, 16), (1, 8)))
    expert_ids_keys = jax.random.split(jax.random.fold_in(seeds[2], 1), TOKENS // TOK_DEV)
    expert_ids_turns = jax.random.permutation(jax.random.fold_in(seeds[2], 3), TOKENS // TOK_DEV)
    expert_ids = jax.vmap(lambda own, number: deal_out(jax.random.fold_in(seeds[2], 2), own, number, TOK_DEV, EXPERTS, TOPK, CAP, 2))(expert_ids_keys, expert_ids_turns).reshape((TOKENS, TOPK))
    gate_values = jnp.clip(0.2 + 0.8 * jax.random.uniform(seeds[3], (TOKENS, TOPK), jnp.float32) ** shard_levels(seeds[3], (TOKENS, TOPK), ((0, 16),), -0.2, 0.2), 0.2, 1.0)
    gate_weight = bell_draw(seeds[4], (EXPERTS, D, FF), D ** -0.5, 0.0625, ((0, 16), (2, 8)))
    up_weight = bell_draw(seeds[5], (EXPERTS, D, FF), D ** -0.5, 0.0625, ((0, 16), (2, 8)))
    down_weight = bell_draw(seeds[6], (EXPERTS, FF, D), FF ** -0.5, 0.1875, ((0, 16), (1, 8)))
    return {"tokens": tokens, "upstream": upstream, "expert_ids": expert_ids, "gate_values": gate_values, "gate_weight": gate_weight, "up_weight": up_weight, "down_weight": down_weight}


def route_slots(expert_ids):
    slot_count = EXP_DEV + 1
    total_slots = N_EXPERT * slot_count
    token_index = jnp.broadcast_to(jnp.arange(TOKENS, dtype=jnp.int32)[:, None], expert_ids.shape)
    resident = (expert_ids // EXP_DEV) * slot_count + expert_ids % EXP_DEV
    local_replica = (token_index // TOK_DEV) * slot_count + EXP_DEV
    target = jnp.where(expert_ids == 0, local_replica, resident).astype(jnp.int32)
    blocks = target.reshape(N_EXPERT, TOK_DEV * TOPK)
    onehot = (blocks[:, :, None] == jnp.arange(total_slots, dtype=jnp.int32)[None, None, :]).astype(jnp.int32)
    earlier = jnp.cumsum(onehot, axis=1) - onehot
    position = jnp.sum(onehot * earlier, axis=2).reshape(TOKENS, TOPK).astype(jnp.int32)
    return target, position


def summed_rounding(partials):
    rounded = lax.optimization_barrier(partials.astype(jnp.bfloat16))
    return jnp.sum(rounded.astype(jnp.float32), axis=0).astype(jnp.bfloat16)


def slot_work(inputs, cotangent, w_gate, w_up, w_down):
    rows = inputs.shape[0]
    gate_pre = jnp.dot(inputs, w_gate, preferred_element_type=jnp.float32)
    up_pre = jnp.dot(inputs, w_up, preferred_element_type=jnp.float32)
    sigmoid_gate = jax.nn.sigmoid(gate_pre)
    activated = gate_pre * sigmoid_gate
    hidden = (activated * up_pre).astype(jnp.bfloat16)
    hidden_groups = hidden.astype(jnp.float32).reshape(rows, N_DP, HID_DEV)
    down_groups = w_down.astype(jnp.float32).reshape(N_DP, HID_DEV, D)
    partials = jnp.einsum("rpf,pfd->prd", hidden_groups, down_groups, precision=lax.Precision.HIGHEST)
    output_rows = summed_rounding(partials)
    hidden_cotangent = jnp.dot(cotangent, w_down.T, preferred_element_type=jnp.float32)
    gate_diff = (hidden_cotangent * up_pre * sigmoid_gate * (1.0 + gate_pre * (1.0 - sigmoid_gate))).astype(jnp.bfloat16)
    up_diff = (hidden_cotangent * activated).astype(jnp.bfloat16)
    gate_groups = w_gate.astype(jnp.float32).reshape(D, N_DP, HID_DEV)
    up_groups = w_up.astype(jnp.float32).reshape(D, N_DP, HID_DEV)
    input_partials = jnp.einsum("rpf,dpf->prd", gate_diff.astype(jnp.float32).reshape(rows, N_DP, HID_DEV), gate_groups, precision=lax.Precision.HIGHEST)
    input_partials = input_partials + jnp.einsum("rpf,dpf->prd", up_diff.astype(jnp.float32).reshape(rows, N_DP, HID_DEV), up_groups, precision=lax.Precision.HIGHEST)
    input_rows = summed_rounding(input_partials)
    grad_gate = jnp.dot(inputs.T, gate_diff, preferred_element_type=jnp.float32)
    grad_up = jnp.dot(inputs.T, up_diff, preferred_element_type=jnp.float32)
    grad_down = jnp.dot(hidden.T, cotangent, preferred_element_type=jnp.float32)
    return output_rows, input_rows, grad_gate, grad_up, grad_down


def reference(tokens, upstream, expert_ids, gate_values, gate_weight, up_weight, down_weight):
    slot_count = EXP_DEV + 1
    total_slots = N_EXPERT * slot_count
    slot_rows = N_EXPERT * CAP
    target, position = route_slots(expert_ids)
    token_ids = jnp.broadcast_to(jnp.arange(TOKENS, dtype=jnp.int32)[:, None], expert_ids.shape)
    route_ids = jnp.arange(TOKENS * TOPK, dtype=jnp.int32).reshape(TOKENS, TOPK)
    row_index = (token_ids // TOK_DEV) * CAP + position
    token_at = jnp.full((total_slots, slot_rows), TOKENS, jnp.int32).at[target, row_index].set(token_ids)
    route_at = jnp.full((total_slots, slot_rows), TOKENS * TOPK, jnp.int32).at[target, row_index].set(route_ids)
    padded_inputs = jnp.concatenate([tokens, jnp.zeros((1, D), jnp.bfloat16)], axis=0)
    scaled = (gate_values[:, :, None] * upstream[:, None, :].astype(jnp.float32)).astype(jnp.bfloat16).reshape(TOKENS * TOPK, D)
    padded_cotangent = jnp.concatenate([scaled, jnp.zeros((1, D), jnp.bfloat16)], axis=0)
    hot_gate = gate_weight[0]
    hot_up = up_weight[0]
    hot_down = down_weight[0]

    def replica_step(totals, column):
        slot = column * slot_count + EXP_DEV
        output_rows, input_rows, grad_gate, grad_up, grad_down = slot_work(padded_inputs[token_at[slot]], padded_cotangent[route_at[slot]], hot_gate, hot_up, hot_down)
        rounded_gate = lax.optimization_barrier(grad_gate.astype(jnp.bfloat16)).astype(jnp.float32)
        rounded_up = lax.optimization_barrier(grad_up.astype(jnp.bfloat16)).astype(jnp.float32)
        rounded_down = lax.optimization_barrier(grad_down.astype(jnp.bfloat16)).astype(jnp.float32)
        return (totals[0] + rounded_gate, totals[1] + rounded_up, totals[2] + rounded_down), (output_rows, input_rows)

    start = (jnp.zeros((D, FF), jnp.float32), jnp.zeros((D, FF), jnp.float32), jnp.zeros((FF, D), jnp.float32))
    replica_sums, replica_results = lax.scan(replica_step, start, jnp.arange(N_EXPERT, dtype=jnp.int32))
    sum_gate, sum_up, sum_down = replica_sums
    replica_out, replica_in = replica_results

    def resident_step(expert):
        slot = (expert // EXP_DEV) * slot_count + expert % EXP_DEV
        output_rows, input_rows, grad_gate, grad_up, grad_down = slot_work(padded_inputs[token_at[slot]], padded_cotangent[route_at[slot]], gate_weight[expert], up_weight[expert], down_weight[expert])
        owner = (expert == 0).astype(jnp.float32)
        return (output_rows, input_rows, (grad_gate + owner * sum_gate).astype(jnp.bfloat16), (grad_up + owner * sum_up).astype(jnp.bfloat16), (grad_down + owner * sum_down).astype(jnp.bfloat16))

    resident_out, resident_in, gate_grad, up_grad, down_grad = lax.map(resident_step, jnp.arange(EXPERTS, dtype=jnp.int32))
    all_out = jnp.concatenate([resident_out.reshape(N_EXPERT, EXP_DEV, slot_rows, D), replica_out[:, None]], axis=1).reshape(total_slots, slot_rows, D)
    all_in = jnp.concatenate([resident_in.reshape(N_EXPERT, EXP_DEV, slot_rows, D), replica_in[:, None]], axis=1).reshape(total_slots, slot_rows, D)
    route_out = all_out[target, row_index]
    route_in = all_in[target, row_index]
    mixed = jnp.sum(gate_values[:, :, None] * route_out.astype(jnp.float32), axis=1).astype(jnp.bfloat16)
    token_grads = jnp.sum(route_in.astype(jnp.float32), axis=1).astype(jnp.bfloat16)
    return (mixed, token_grads, gate_grad, up_grad, down_grad)
```

```python
import jax
import jax.numpy as jnp
from jax import lax
from jax.experimental import pallas as pl
from jax.experimental.pallas import tpu as pltpu
from jax.sharding import PartitionSpec as P

BF = jnp.bfloat16
F32 = jnp.float32
LOW, HIGH = 80, 176
PARAMS = pltpu.CompilerParams(vmem_limit_bytes=48 * 1024 * 1024)


def dot(a, b, dims=((1,), (0,)), precision=None):
    return lax.dot_general(a, b, (dims, ((), ())), precision=precision, preferred_element_type=F32)


def dispatch_kernel(ids_ref, gates_ref, tokens_ref, upstream_ref, rows_ref, pick_ref, gated_ref):
    count, top = ids_ref.shape
    total = rows_ref.shape[0]
    width = tokens_ref.shape[1]
    capacity = 8
    row = lax.broadcasted_iota(jnp.int32, (count, total), 1)
    expert = row // capacity
    named = jnp.zeros((count, total), F32)
    gate = jnp.zeros((count, total), F32)
    for k in range(top):
        hit = ids_ref[:, k : k + 1] == expert
        named = jnp.where(hit, 1.0, named)
        gate = jnp.where(hit, gates_ref[:, k : k + 1], gate)
    later = lax.broadcasted_iota(jnp.int32, (count, count), 0)
    sooner = lax.broadcasted_iota(jnp.int32, (count, count), 1)
    earlier = jnp.where(sooner < later, 1.0, 0.0)
    position = dot(earlier.astype(BF), named.astype(BF))
    chosen = (named > 0.5) & (position == (row % capacity).astype(F32))
    pick = jnp.where(chosen, 1.0, 0.0)
    gated = jnp.where(chosen, gate, 0.0)
    pick_ref[...] = pick.astype(BF)
    gated_ref[...] = gated
    rows_ref[:, :width] = dot(pick.astype(BF), tokens_ref[...], ((0,), (0,))).astype(BF)
    rows_ref[:, width:] = dot(
        gated, upstream_ref[...].astype(F32), ((0,), (0,)), lax.Precision.HIGHEST
    ).astype(BF)


def dispatch(ids, gates, tokens, upstream, total):
    count, width = tokens.shape
    return pl.pallas_call(
        dispatch_kernel,
        out_shape=(
            jax.ShapeDtypeStruct((total, 2 * width), BF),
            jax.ShapeDtypeStruct((count, total), BF),
            jax.ShapeDtypeStruct((count, total), F32),
        ),
        compiler_params=PARAMS,
        name="dispatch",
    )(ids, gates, tokens, upstream)


class Links:
    def __init__(self, size):
        rings = size // 2
        self.up = [(z * 2 + x, (z + 1) % rings * 2 + x) for z in range(rings) for x in range(2)]
        self.down = [(z * 2 + x, (z - 1) % rings * 2 + x) for z in range(rings) for x in range(2)]
        self.side = [(i, i ^ 1) for i in range(size)]

    def send_up(self, value):
        return lax.ppermute(value, "dp", self.up)

    def send_down(self, value):
        return lax.ppermute(value, "dp", self.down)

    def cross(self, value):
        return lax.ppermute(value, "dp", self.side)


def gather(links, own):
    above = links.send_down(own)
    below = links.send_up(own)
    beside = links.cross(own)
    above2 = links.send_down(jnp.concatenate([above[:HIGH], beside[:LOW]]))
    below2 = links.send_up(jnp.concatenate([below[HIGH:], beside[LOW:]]))
    beside2 = links.cross(jnp.concatenate([above[LOW:], below[:LOW]]))
    above3 = links.send_down(above2[HIGH:])
    beside3 = links.cross(above2[LOW:HIGH])
    below3 = links.send_up(below2[HIGH:])
    return (own, above, below, beside, above2, below2, beside2, above3, beside3, below3)


PIECES = 10


def assemble(pieces, full_ref):
    own, above, below, beside, above2, below2, beside2, above3, beside3, below3 = pieces
    full_ref[0] = own[...]
    full_ref[1] = above[...]
    full_ref[2] = below[...]
    full_ref[3] = beside[...]
    full_ref[4, :HIGH] = above2[:HIGH]
    full_ref[4, HIGH:] = below2[:LOW]
    full_ref[5, :LOW] = above2[HIGH:]
    full_ref[5, LOW:] = beside2[:HIGH]
    full_ref[6, :LOW] = beside2[HIGH:]
    full_ref[6, LOW:] = below2[LOW:]
    full_ref[7, :LOW] = above3[...]
    full_ref[7, LOW:HIGH] = beside3[...]
    full_ref[7, HIGH:] = below3[...]


def block_order():
    me = lax.axis_index("dp")
    rings = lax.axis_size("dp") // 2
    z, x = me // 2, me % 2
    steps = ((0, 0), (1, 0), (-1, 0), (0, 1), (2, 0), (1, 1), (-1, 1), (2, 1))
    return jnp.stack([(z + dz + rings) % rings * 2 + (x + dx) % 2 for dz, dx in steps]).astype(
        jnp.int32
    )


def store_partials(step, value, outs):
    cut_up, cut_side, cut_down = outs[:3]

    @pl.when(step == 7)
    def _():
        cut_up[...] = value[:LOW]
        cut_side[...] = value[LOW:HIGH]
        cut_down[...] = value[HIGH:]

    for block in range(7):

        @pl.when(step == block)
        def _(block=block):
            outs[3 + block][...] = value


def partial_shapes(rows, width):
    sizes = (LOW, HIGH - LOW, rows - HIGH) + (rows,) * 7
    return tuple(jax.ShapeDtypeStruct((size, width), BF) for size in sizes)


def row_slot(shape):
    return lax.broadcasted_iota(jnp.int32, shape, 0) // 8 % 2 == 0


def pair(first, value):
    zero = jnp.zeros_like(value)
    return jnp.concatenate([jnp.where(first, value, zero), jnp.where(first, zero, value)], axis=1)


def whole(array):
    return pl.BlockSpec(array.shape, lambda j, order, n=len(array.shape): (0,) * n)


def forward_kernel(order_ref, *refs):
    pieces, refs = refs[:PIECES], refs[PIECES:]
    gate_ref, up_ref, down_ref = refs[:3]
    full_ref, pre_ref, hidden_ref = refs[3:6]
    partials = refs[6:16]
    step = pl.program_id(0)
    half = pre_ref.shape[1] // 2

    @pl.when(step == 0)
    def _():
        assemble(pieces, full_ref)

    @pl.when(step < 8)
    def _():
        rows = full_ref[step]
        gate = dot(rows, jnp.concatenate([gate_ref[0], gate_ref[1]], axis=1))
        up = dot(rows, jnp.concatenate([up_ref[0], up_ref[1]], axis=1))
        first = row_slot((rows.shape[0], half))
        gate = jnp.where(first, gate[:, :half], gate[:, half:])
        up = jnp.where(first, up[:, :half], up[:, half:])

        @pl.when(step == 0)
        def _():
            pre_ref[:, :half] = gate
            pre_ref[:, half:] = up

        @pl.when(step > 0)
        def _():
            pre_ref[:, :half] += gate
            pre_ref[:, half:] += up

    @pl.when(step == 7)
    def _():
        gate = pre_ref[:, :half]
        hidden = (gate * jax.nn.sigmoid(gate) * pre_ref[:, half:]).astype(BF)
        hidden_ref[...] = pair(row_slot(hidden.shape), hidden)

    @pl.when(step >= 8)
    def _():
        store_partials(step - 8, dot(hidden_ref[...], down_ref[...]).astype(BF), partials)


def forward(order, pieces, gate_weight, up_weight, down_flat):
    rows, width = pieces[0].shape
    hid = gate_weight.shape[2]
    first = lambda j, order: (0, order[jnp.minimum(j, 7)], 0)
    second = lambda j, order: (0, order[jnp.maximum(j - 8, 0)])
    shapes = (
        jax.ShapeDtypeStruct((8, rows, width), BF),
        jax.ShapeDtypeStruct((rows, 2 * hid), F32),
        jax.ShapeDtypeStruct((rows, 2 * hid), BF),
    ) + partial_shapes(rows, width)
    out = pl.pallas_call(
        forward_kernel,
        grid_spec=pltpu.PrefetchScalarGridSpec(
            num_scalar_prefetch=1,
            grid=(16,),
            in_specs=[whole(p) for p in pieces]
            + [
                pl.BlockSpec((2, width, hid), first),
                pl.BlockSpec((2, width, hid), first),
                pl.BlockSpec((2 * hid, width), second),
            ],
            out_specs=[whole(s) for s in shapes],
        ),
        out_shape=shapes,
        compiler_params=PARAMS,
        name="forward",
    )(order, *pieces, gate_weight, up_weight, down_flat)
    return out[0], out[1], out[2], out[3:]


def backward_kernel(order_ref, *refs):
    pieces, refs = refs[:PIECES], refs[PIECES:]
    pre_ref, gate_ref, up_ref, down_ref = refs[:4]
    full_ref, gate_diff_ref, up_diff_ref = refs[4:7]
    partials = refs[7:17]
    acc_ref = refs[17]
    step = pl.program_id(0)
    half = pre_ref.shape[1] // 2

    @pl.when(step == 0)
    def _():
        assemble(pieces, full_ref)

    @pl.when(step < 8)
    def _():
        part = dot(full_ref[step], down_ref[...], ((1,), (1,)))

        @pl.when(step == 0)
        def _():
            acc_ref[...] = part

        @pl.when(step > 0)
        def _():
            acc_ref[...] += part

    @pl.when(step == 7)
    def _():
        first = row_slot((acc_ref.shape[0], half))
        cotangent = jnp.where(first, acc_ref[:, :half], acc_ref[:, half:])
        gate, up = pre_ref[:, :half], pre_ref[:, half:]
        sigmoid = jax.nn.sigmoid(gate)
        gate_diff = (cotangent * up * sigmoid * (1.0 + gate * (1.0 - sigmoid))).astype(BF)
        up_diff = (cotangent * (gate * sigmoid)).astype(BF)
        gate_diff_ref[...] = pair(first, gate_diff)
        up_diff_ref[...] = pair(first, up_diff)

    @pl.when(step >= 8)
    def _():
        nt = ((1,), (1,))
        value = dot(gate_diff_ref[...], jnp.concatenate([gate_ref[0], gate_ref[1]], axis=1), nt)
        value += dot(up_diff_ref[...], jnp.concatenate([up_ref[0], up_ref[1]], axis=1), nt)
        store_partials(step - 8, value.astype(BF), partials)


def backward(order, pieces, pre, gate_weight, up_weight, down_flat):
    rows, width = pieces[0].shape
    hid = gate_weight.shape[2]
    first = lambda j, order: (0, order[jnp.minimum(j, 7)])
    second = lambda j, order: (0, order[jnp.maximum(j - 8, 0)], 0)
    shapes = (
        jax.ShapeDtypeStruct((8, rows, width), BF),
        jax.ShapeDtypeStruct((rows, 2 * hid), BF),
        jax.ShapeDtypeStruct((rows, 2 * hid), BF),
    ) + partial_shapes(rows, width)
    out = pl.pallas_call(
        backward_kernel,
        grid_spec=pltpu.PrefetchScalarGridSpec(
            num_scalar_prefetch=1,
            grid=(16,),
            in_specs=[whole(p) for p in pieces]
            + [
                whole(pre),
                pl.BlockSpec((2, width, hid), second),
                pl.BlockSpec((2, width, hid), second),
                pl.BlockSpec((2 * hid, width), first),
            ],
            out_specs=[whole(s) for s in shapes],
            scratch_shapes=[pltpu.VMEM((rows, 2 * hid), F32)],
        ),
        out_shape=shapes,
        compiler_params=PARAMS,
        name="backward",
    )(order, *pieces, pre, gate_weight, up_weight, down_flat)
    return out[0], out[1], out[2], out[3:]


def weights_kernel(
    order_ref, x_ref, c_ref, hidden_ref, gate_diff_ref, up_diff_ref, gate_out, up_out, down_out
):
    tn = ((0,), (0,))
    hid = gate_out.shape[2]
    for diff_ref, out_ref in ((gate_diff_ref, gate_out), (up_diff_ref, up_out)):
        grad = dot(x_ref[0], diff_ref[...], tn).astype(BF)
        out_ref[0] = grad[:, :hid]
        out_ref[1] = grad[:, hid:]
    down_out[...] = dot(hidden_ref[...], c_ref[0], tn).astype(BF)


def weight_grads(order, x_full, c_full, hidden, gate_diff, up_diff):
    blocks, rows, width = x_full.shape
    hid = hidden.shape[1] // 2
    block = pl.BlockSpec((1, rows, width), lambda j, order: (j, 0, 0))
    grad = pl.BlockSpec((2, width, hid), lambda j, order: (0, order[j], 0))
    return pl.pallas_call(
        weights_kernel,
        grid_spec=pltpu.PrefetchScalarGridSpec(
            num_scalar_prefetch=1,
            grid=(blocks,),
            in_specs=[block, block, whole(hidden), whole(gate_diff), whole(up_diff)],
            out_specs=[
                grad,
                grad,
                pl.BlockSpec((2 * hid, width), lambda j, order: (0, order[j])),
            ],
        ),
        out_shape=(
            jax.ShapeDtypeStruct((2, blocks * width, hid), BF),
            jax.ShapeDtypeStruct((2, blocks * width, hid), BF),
            jax.ShapeDtypeStruct((2 * hid, blocks * width), BF),
        ),
        compiler_params=PARAMS,
        name="weight_grads",
    )(order, x_full, c_full, hidden, gate_diff, up_diff)


def add(a, b):
    return (a.astype(F32) + b.astype(F32)).astype(BF)


def second_hop_kernel(far, above1, below1, got_up, got_side, got_down, to_up, to_down, to_side):
    to_up[:LOW] = far[:LOW]
    to_up[LOW:HIGH] = add(far[LOW:HIGH], got_side[...])
    to_up[HIGH:] = add(above1[:LOW], got_up[...])
    to_down[:LOW] = far[HIGH:]
    to_down[LOW:HIGH] = below1[LOW:HIGH]
    to_down[HIGH:] = add(below1[HIGH:], got_down[...])
    to_side[:HIGH] = above1[LOW:]
    to_side[HIGH:] = below1[:LOW]


def third_hop_kernel(above, below, beside, got_up, got_down, got_side, to_up, to_down, to_side):
    to_up[:LOW] = add(above[:LOW], got_up[:LOW])
    to_up[LOW:HIGH] = (
        above[LOW:HIGH].astype(F32)
        + got_up[LOW:HIGH].astype(F32)
        + got_side[: HIGH - LOW].astype(F32)
    ).astype(BF)
    to_up[HIGH:] = add(above[HIGH:], got_side[HIGH - LOW : HIGH])
    to_down[:LOW] = add(below[:LOW], got_side[HIGH:])
    to_down[LOW:HIGH] = below[LOW:HIGH]
    to_down[HIGH:] = add(below[HIGH:], got_down[:LOW])
    to_side[:LOW] = add(beside[:LOW], got_up[HIGH:])
    to_side[LOW:] = add(beside[LOW:], got_down[LOW:])


def last_kernel(own, from_below, from_above, from_side, total):
    total[...] = (
        (own[...].astype(F32) + from_side[...].astype(F32))
        + (from_below[...].astype(F32) + from_above[...].astype(F32))
    ).astype(BF)


def local_call(kernel, name, count, *args):
    shape = jax.ShapeDtypeStruct(args[0].shape, BF)
    return pl.pallas_call(
        kernel,
        out_shape=(shape,) * count if count > 1 else shape,
        compiler_params=PARAMS,
        name=name,
    )(*args)


def reduce_scatter(links, partials):
    cut_up, cut_side, cut_down, own, above, below, beside, far, above1, below1 = partials
    got_up = links.send_up(cut_up)
    got_side = links.cross(cut_side)
    got_down = links.send_down(cut_down)
    to_up, to_down, to_side = local_call(
        second_hop_kernel, "second_hop", 3, far, above1, below1, got_up, got_side, got_down
    )
    got_up = links.send_up(to_up)
    got_down = links.send_down(to_down)
    got_side = links.cross(to_side)
    to_up, to_down, to_side = local_call(
        third_hop_kernel, "third_hop", 3, above, below, beside, got_up, got_down, got_side
    )
    got_up = links.send_up(to_up)
    got_down = links.send_down(to_down)
    got_side = links.cross(to_side)
    return local_call(last_kernel, "last_hop", 1, own, got_up, got_down, got_side)


def combine_kernel(pick_ref, gated_ref, out_ref, in_ref, mixed_ref, grads_ref):
    mixed_ref[...] = dot(
        gated_ref[...], out_ref[...].astype(F32), precision=lax.Precision.HIGHEST
    ).astype(BF)
    grads_ref[...] = dot(pick_ref[...], in_ref[...]).astype(BF)


def on_device(tokens, upstream, expert_ids, gate_values, gate_weight, up_weight, down_weight):
    columns = lax.axis_size("expert")
    exp_dev, hid, features = down_weight.shape
    rows = columns * exp_dev * 8
    width = tokens.shape[1]
    links = Links(lax.axis_size("dp"))
    order = block_order()
    down_flat = down_weight.reshape(exp_dev * hid, features)

    outgoing, pick, gated = dispatch(expert_ids, gate_values, tokens, upstream, rows)
    arrived = lax.all_to_all(
        outgoing.reshape(columns, exp_dev * 8, 2 * width), "expert", 0, 0, tiled=True
    ).reshape(rows, 2 * width)
    x_pieces = gather(links, arrived[:, :width])
    c_pieces = gather(links, arrived[:, width:])
    x_full, pre, hidden, out_partials = forward(order, x_pieces, gate_weight, up_weight, down_flat)
    out_rows = reduce_scatter(links, out_partials)
    c_full, gate_diff, up_diff, in_partials = backward(
        order, c_pieces, pre, gate_weight, up_weight, down_flat
    )
    in_rows = reduce_scatter(links, in_partials)
    gate_grad, up_grad, down_grad = weight_grads(
        order, x_full, c_full, hidden, gate_diff, up_diff
    )

    def give_back(value):
        return lax.all_to_all(
            value.reshape(columns, exp_dev * 8, width), "expert", 0, 0, tiled=True
        ).reshape(rows, width)

    shape = jax.ShapeDtypeStruct(tokens.shape, BF)
    mixed, token_grads = pl.pallas_call(
        combine_kernel, out_shape=(shape, shape), compiler_params=PARAMS, name="combine"
    )(pick, gated, give_back(out_rows), give_back(in_rows))
    return (mixed, token_grads, gate_grad, up_grad, down_grad.reshape(down_weight.shape))


def solution(mesh):
    return jax.shard_map(
        on_device,
        mesh=mesh,
        in_specs=(
            P("expert", "dp"),
            P("expert", "dp"),
            P("expert", None),
            P("expert", None),
            P("expert", None, "dp"),
            P("expert", None, "dp"),
            P("expert", "dp", None),
        ),
        out_specs=(
            P("expert", "dp"),
            P("expert", "dp"),
            P("expert", None, "dp"),
            P("expert", None, "dp"),
            P("expert", "dp", None),
        ),
        check_vma=False,
    )
```

```python
import jax
import jax.numpy as jnp
from jax import lax
from jax.experimental import pallas as pl
from jax.experimental.pallas import tpu as pltpu
from jax.sharding import PartitionSpec as P

BF = jnp.bfloat16
F32 = jnp.float32
LOW, HALF, HIGH = 112, 128, 144
ARRIVING = ((0, 1, 2, 3), (4, 5, 6), (7,))
LEAVING = ((7,), (4, 5, 6), (1, 2, 3, 0))
MIB = 1024 * 1024
SMALL = pltpu.CompilerParams(vmem_limit_bytes=8 * MIB)
LARGE = pltpu.CompilerParams(vmem_limit_bytes=16 * MIB)
HBM = pl.BlockSpec(memory_space=pl.ANY)
VMEM = pl.BlockSpec(memory_space=pltpu.VMEM)
SMEM = pl.BlockSpec(memory_space=pltpu.SMEM)


def dot(a, b, dims=((1,), (0,)), precision=None):
    return lax.dot_general(a, b, (dims, ((), ())), precision=precision, preferred_element_type=F32)


def in_hbm(value):
    return pltpu.with_memory_space_constraint(value, pltpu.HBM)


class Copies:
    def __init__(self, semaphores):
        self.semaphores = semaphores
        self.used = 0

    def start(self, pairs):
        started = []
        for source, target in pairs:
            started.append(pltpu.make_async_copy(source, target, self.semaphores.at[self.used]))
            started[-1].start()
            self.used += 1
        return started


def wait(copies):
    for copy in copies:
        copy.wait()


def dispatch_kernel(
    ids_hbm, gates_hbm, tokens_ref, upstream_ref, x_ref, c_ref, pick_ref, gated_ref,
    ids_ref, gates_ref, held, semaphores,
):
    copies = Copies(semaphores)
    routes = copies.start(((ids_hbm, ids_ref), (gates_hbm, gates_ref)))
    arriving = copies.start(((tokens_ref, held.at[0]), (upstream_ref, held.at[1])))
    total, count = pick_ref.shape
    capacity = 8
    row = lax.broadcasted_iota(jnp.int32, (total, count), 0)
    expert = row // capacity
    wait(routes)
    named = jnp.zeros((total, count), F32)
    gate = jnp.zeros((total, count), F32)
    for k in range(ids_ref.shape[0]):
        hit = ids_ref[k : k + 1, :] == expert
        named = jnp.where(hit, 1.0, named)
        gate = jnp.where(hit, gates_ref[k : k + 1, :], gate)
    sooner = lax.broadcasted_iota(jnp.int32, (count, count), 0)
    later = lax.broadcasted_iota(jnp.int32, (count, count), 1)
    earlier = jnp.where(sooner < later, 1.0, 0.0)
    position = dot(named.astype(BF), earlier.astype(BF))
    chosen = (named > 0.5) & (position == (row % capacity).astype(F32))
    pick = jnp.where(chosen, 1.0, 0.0).astype(BF)
    gated = jnp.where(chosen, gate, 0.0)
    pick_ref[...] = pick
    gated_ref[...] = gated
    wait(arriving)
    x_ref[...] = dot(pick, held[0]).astype(BF)
    c_ref[...] = dot(gated, held[1].astype(F32), precision=lax.Precision.HIGHEST).astype(BF)


def dispatch(ids, gates, tokens, upstream, total):
    count, width = tokens.shape
    return pl.pallas_call(
        dispatch_kernel,
        in_specs=[HBM] * 4,
        out_shape=(
            jax.ShapeDtypeStruct((total, width), BF),
            jax.ShapeDtypeStruct((total, width), BF),
            jax.ShapeDtypeStruct((total, count), BF),
            jax.ShapeDtypeStruct((total, count), F32),
        ),
        scratch_shapes=[
            pltpu.VMEM((ids.shape[1], count), jnp.int32),
            pltpu.VMEM((ids.shape[1], count), F32),
            pltpu.VMEM((2, count, width), BF),
            pltpu.SemaphoreType.DMA((4,)),
        ],
        compiler_params=SMALL,
        name="dispatch",
    )(*[in_hbm(value) for value in (ids.T, gates.T, tokens, upstream)])


class Links:
    def __init__(self, size):
        rings = size // 2
        self.up = [(z * 2 + x, (z + 1) % rings * 2 + x) for z in range(rings) for x in range(2)]
        self.down = [(z * 2 + x, (z - 1) % rings * 2 + x) for z in range(rings) for x in range(2)]
        self.side = [(i, i ^ 1) for i in range(size)]

    def send_up(self, value):
        return lax.ppermute(value, "dp", self.up)

    def send_down(self, value):
        return lax.ppermute(value, "dp", self.down)

    def cross(self, value):
        return lax.ppermute(value, "dp", self.side)


def after(value, *earlier):
    return lax.optimization_barrier((value, *earlier))[0]


def local_call(kernel, name, sizes, *args):
    width = args[0].shape[1]
    shapes = tuple(jax.ShapeDtypeStruct((size, width), BF) for size in sizes)
    return pl.pallas_call(kernel, out_shape=shapes, compiler_params=SMALL, name=name)(*args)


def relay_kernel(above, below, beside, to_down, to_up, to_side):
    to_down[:HALF] = above[:HALF]
    to_down[HALF:] = beside[:LOW]
    to_up[:HALF] = below[HALF:]
    to_up[HALF:] = beside[HIGH:]
    to_side[:HIGH] = above[LOW:]
    to_side[HIGH:] = below[:HIGH]


def ends_kernel(above2, below2, beside2, to_down, to_up):
    to_down[:LOW] = above2[HALF:]
    to_down[LOW:] = beside2[: HALF - LOW]
    to_up[: HALF - LOW] = beside2[HIGH + HALF :]
    to_up[HALF - LOW :] = below2[HALF:]


class Gather:
    def __init__(self, links, own):
        self.links = links
        self.arrived = [(own, links.send_down(own), links.send_up(own), links.cross(own))]

    def relay(self, *earlier):
        links = self.links
        outgoing = local_call(
            relay_kernel,
            "relay",
            (HALF + LOW, HALF + LOW, 2 * HIGH),
            *after(self.arrived[0][1:], *earlier),
        )
        to_down, to_up, to_side = outgoing
        self.arrived.append(
            (links.send_down(to_down), links.send_up(to_up), links.cross(to_side))
        )
        return outgoing

    def ends(self, *earlier):
        links = self.links
        outgoing = local_call(ends_kernel, "ends", (HALF, HALF), *after(self.arrived[1], *earlier))
        self.arrived.append((links.send_down(outgoing[0]), links.send_up(outgoing[1])))
        return outgoing


def arrived_blocks(part, pieces):
    if part == 0:
        return [piece[...] for piece in pieces]
    stack = lambda a, b: jnp.concatenate([a, b], axis=0)
    if part == 1:
        above2, below2, beside2 = pieces
        return [
            stack(above2[:HALF], below2[:HALF]),
            stack(above2[HALF:], beside2[:HIGH]),
            stack(beside2[HIGH:], below2[HALF:]),
        ]
    return [stack(pieces[0][...], pieces[1][...])]


def block_order():
    me = lax.axis_index("dp")
    rings = lax.axis_size("dp") // 2
    z, x = me // 2, me % 2
    steps = ((0, 0), (1, 0), (-1, 0), (0, 1), (2, 0), (1, 1), (-1, 1), (2, 1))
    return jnp.stack([(z + dz + rings) % rings * 2 + (x + dx) % 2 for dz, dx in steps]).astype(
        jnp.int32
    )


def row_slot(shape):
    return lax.broadcasted_iota(jnp.int32, shape, 0) // 8 % 2 == 0


def pair(first, value):
    zero = jnp.zeros_like(value)
    return jnp.concatenate([jnp.where(first, value, zero), jnp.where(first, zero, value)], axis=1)


def features_of(order_ref, block, width):
    return pl.ds(pl.multiple_of(order_ref[block] * width, 128), width)


def load_columns(copies, order_ref, refs, buffers, blocks):
    width = buffers[0].shape[2]
    return [
        copies.start(
            [
                (ref.at[:, features_of(order_ref, block, width), :], buffer.at[i])
                for ref, buffer in zip(refs, buffers)
            ]
        )
        for i, block in enumerate(blocks)
    ]


def load_rows(copies, order_ref, ref, buffer, blocks):
    width = buffer.shape[2]
    return [
        copies.start([(ref.at[:, features_of(order_ref, block, width)], buffer.at[i])])
        for i, block in enumerate(blocks)
    ]


def both(ref, i):
    return jnp.concatenate([ref[i, 0], ref[i, 1]], axis=1)


def column_buffers(blocks, width, hid):
    return [pltpu.VMEM((len(blocks), 2, width, hid), BF)] * 2


def row_buffers(blocks, width, hid):
    return [pltpu.VMEM((len(blocks), 2 * hid, width), BF)]


def semaphores_for(blocks, each):
    return [pltpu.SemaphoreType.DMA((each * len(blocks),))]


NT = ((1,), (1,))
TN = ((0,), (0,))


def gate_up(part, order, pieces, weights, before=None):
    blocks = ARRIVING[part]
    rows, width = 2 * HALF, pieces[0].shape[1]
    hid = weights[0].shape[2]
    last = part == len(ARRIVING) - 1

    def kernel(order_ref, *refs):
        count = len(pieces)
        held_pieces, refs = refs[:count], refs[count:]
        if before is not None:
            before_ref, refs = refs[0], refs[1:]
        columns, pre_ref, refs = refs[:2], refs[2], refs[3:]
        if last:
            hidden_ref, refs = refs[0], refs[1:]
        gate_held, up_held, semaphores = refs
        arriving = load_columns(
            Copies(semaphores), order_ref, columns, (gate_held, up_held), blocks
        )
        first = row_slot((rows, hid))
        for i, value in enumerate(arrived_blocks(part, held_pieces)):
            wait(arriving[i])
            gate = dot(value, both(gate_held, i))
            up = dot(value, both(up_held, i))
            gate = jnp.where(first, gate[:, :hid], gate[:, hid:])
            up = jnp.where(first, up[:, :hid], up[:, hid:])
            so_far = pre_ref if i else before_ref if before is not None else None
            if so_far is not None:
                gate += so_far[:, :hid]
                up += so_far[:, hid:]
            pre_ref[:, :hid] = gate
            pre_ref[:, hid:] = up
        if last:
            gate = pre_ref[:, :hid]
            hidden = (gate * jax.nn.sigmoid(gate) * pre_ref[:, hid:]).astype(BF)
            hidden_ref[...] = pair(first, hidden)

    shapes = [jax.ShapeDtypeStruct((rows, 2 * hid), F32)]
    if last:
        shapes.append(jax.ShapeDtypeStruct((rows, 2 * hid), BF))
    extra = [] if before is None else [before]
    out = pl.pallas_call(
        kernel,
        in_specs=[SMEM] + [VMEM] * (len(pieces) + len(extra)) + [HBM] * 2,
        out_shape=shapes,
        scratch_shapes=column_buffers(blocks, width, hid) + semaphores_for(blocks, 2),
        compiler_params=LARGE,
        name=f"gate_up_{part}",
    )(order, *pieces, *extra, *weights)
    return out if last else out[0]


def output_sums(part, order, hidden, down_flat, width):
    blocks = LEAVING[part]
    rows, units = hidden.shape

    def kernel(order_ref, hidden_ref, down_ref, *refs):
        outs = refs[:-2]
        down_held, semaphores = refs[-2:]
        arriving = load_rows(Copies(semaphores), order_ref, down_ref, down_held, blocks)
        for i in range(len(blocks)):
            wait(arriving[i])
            store_sum(part, i, dot(hidden_ref[...], down_held[i]).astype(BF), outs)

    return pl.pallas_call(
        kernel,
        in_specs=[SMEM, VMEM, HBM],
        out_shape=sum_shapes(part, rows, width),
        scratch_shapes=row_buffers(blocks, width, units // 2) + semaphores_for(blocks, 1),
        compiler_params=LARGE,
        name=f"output_sums_{part}",
    )(order, hidden, down_flat)


def sum_shapes(part, rows, width):
    sizes = (HALF, HALF) if part == 0 else (rows,) * len(LEAVING[part])
    return [jax.ShapeDtypeStruct((size, width), BF) for size in sizes]


def store_sum(part, i, value, outs):
    if part == 0:
        outs[0][...] = value[:HALF]
        outs[1][...] = value[HALF:]
    else:
        outs[i][...] = value


def cotangents(part, order, pieces, down_flat, before=None, pre=None):
    blocks = ARRIVING[part]
    rows, width = 2 * HALF, pieces[0].shape[1]
    hid = down_flat.shape[0] // 2
    last = part == len(ARRIVING) - 1

    def kernel(order_ref, *refs):
        count = len(pieces)
        held_pieces, refs = refs[:count], refs[count:]
        if before is not None:
            before_ref, refs = refs[0], refs[1:]
        if last:
            pre_ref, refs = refs[0], refs[1:]
        down_ref, outs = refs[0], refs[1:-2]
        down_held, semaphores = refs[-2:]
        arriving = load_rows(Copies(semaphores), order_ref, down_ref, down_held, blocks)
        first = row_slot((rows, hid))
        total = before_ref[...] if before is not None else None
        for i, value in enumerate(arrived_blocks(part, held_pieces)):
            wait(arriving[i])
            share = dot(value, down_held[i], NT)
            share = jnp.where(first, share[:, :hid], share[:, hid:])
            total = share if total is None else total + share
        if not last:
            outs[0][...] = total
            return
        gate, up = pre_ref[:, :hid], pre_ref[:, hid:]
        sigmoid = jax.nn.sigmoid(gate)
        gate_diff = (total * up * sigmoid * (1.0 + gate * (1.0 - sigmoid))).astype(BF)
        up_diff = (total * (gate * sigmoid)).astype(BF)
        outs[0][...] = pair(first, gate_diff)
        outs[1][...] = pair(first, up_diff)

    if last:
        shapes = [jax.ShapeDtypeStruct((rows, 2 * hid), BF)] * 2
    else:
        shapes = [jax.ShapeDtypeStruct((rows, hid), F32)]
    extra = [value for value in (before, pre) if value is not None]
    out = pl.pallas_call(
        kernel,
        in_specs=[SMEM] + [VMEM] * (len(pieces) + len(extra)) + [HBM],
        out_shape=shapes,
        scratch_shapes=row_buffers(blocks, width, hid) + semaphores_for(blocks, 1),
        compiler_params=LARGE,
        name=f"cotangents_{part}",
    )(order, *pieces, *extra, down_flat)
    return out if last else out[0]


def input_sums(part, order, diffs, weights, width):
    blocks = LEAVING[part]
    rows, units = diffs[0].shape

    def kernel(order_ref, gate_diff_ref, up_diff_ref, gate_ref, up_ref, *refs):
        outs = refs[:-3]
        gate_held, up_held, semaphores = refs[-3:]
        arriving = load_columns(
            Copies(semaphores), order_ref, (gate_ref, up_ref), (gate_held, up_held), blocks
        )
        for i in range(len(blocks)):
            wait(arriving[i])
            value = dot(gate_diff_ref[...], both(gate_held, i), NT)
            value += dot(up_diff_ref[...], both(up_held, i), NT)
            store_sum(part, i, value.astype(BF), outs)

    return pl.pallas_call(
        kernel,
        in_specs=[SMEM, VMEM, VMEM, HBM, HBM],
        out_shape=sum_shapes(part, rows, width),
        scratch_shapes=column_buffers(blocks, width, units // 2) + semaphores_for(blocks, 2),
        compiler_params=LARGE,
        name=f"input_sums_{part}",
    )(order, *diffs, *weights)


def all_blocks(pieces):
    at = 0
    for part, count in enumerate((4, 3, 2)):
        for block, value in zip(ARRIVING[part], arrived_blocks(part, pieces[at : at + count])):
            yield block, value
        at += count


def column_grads_kernel(order_ref, *refs):
    pieces = refs[:9]
    diffs, outs, held, semaphores = refs[9:11], refs[11:13], refs[13:15], refs[15]
    width, hid = held[0].shape[2:]
    copies = Copies(semaphores)
    leaving = []
    for block, value in all_blocks(pieces):
        for diff_ref, out_ref, held_ref in zip(diffs, outs, held):
            grad = dot(value, diff_ref[...], TN).astype(BF)
            held_ref[block, 0] = grad[:, :hid]
            held_ref[block, 1] = grad[:, hid:]
            target = out_ref.at[:, features_of(order_ref, block, width), :]
            leaving += copies.start([(held_ref.at[block], target)])
    wait(leaving)


def column_grads(order, pieces, diffs):
    width = pieces[0].shape[1]
    hid = diffs[0].shape[1] // 2
    blocks = range(8)
    return pl.pallas_call(
        column_grads_kernel,
        in_specs=[SMEM] + [VMEM] * 11,
        out_specs=[HBM] * 2,
        out_shape=[jax.ShapeDtypeStruct((2, 8 * width, hid), BF)] * 2,
        scratch_shapes=column_buffers(blocks, width, hid) + semaphores_for(blocks, 2),
        compiler_params=LARGE,
        name="column_grads",
    )(order, *pieces, *diffs)


def row_grads_kernel(order_ref, *refs):
    pieces = refs[:9]
    hidden_ref, down_out, held, semaphores = refs[9:]
    width = held.shape[2]
    copies = Copies(semaphores)
    leaving = []
    for block, value in all_blocks(pieces):
        held[block] = dot(hidden_ref[...], value, TN).astype(BF)
        target = down_out.at[:, features_of(order_ref, block, width)]
        leaving += copies.start([(held.at[block], target)])
    wait(leaving)


def row_grads(order, pieces, hidden):
    width = pieces[0].shape[1]
    units = hidden.shape[1]
    blocks = range(8)
    return pl.pallas_call(
        row_grads_kernel,
        in_specs=[SMEM] + [VMEM] * 10,
        out_specs=HBM,
        out_shape=jax.ShapeDtypeStruct((units, 8 * width), BF),
        scratch_shapes=row_buffers(blocks, width, units // 2) + semaphores_for(blocks, 1),
        compiler_params=LARGE,
        name="row_grads",
    )(order, *pieces, hidden)


def wide(value):
    return value.astype(F32)


def second_hop_kernel(far, above1, below1, got_up, got_down, to_up, to_down, to_side):
    to_up[:HALF] = far[:HALF]
    to_up[HALF:] = (wide(above1[:LOW]) + wide(got_up[:LOW])).astype(BF)
    to_down[:HALF] = far[HALF:]
    to_down[HALF:] = (wide(below1[HIGH:]) + wide(got_down[HIGH - HALF :])).astype(BF)
    cut = HALF - LOW
    to_side[:cut] = (wide(above1[LOW:HALF]) + wide(got_up[LOW:])).astype(BF)
    to_side[cut:HIGH] = above1[HALF:]
    to_side[HIGH : HIGH + HALF] = below1[:HALF]
    to_side[HIGH + HALF :] = (wide(below1[HALF:HIGH]) + wide(got_down[: HIGH - HALF])).astype(BF)


def third_hop_kernel(above, below, beside, got_up, got_down, got_side, to_up, to_down, to_side):
    cut = HALF - LOW
    to_up[:LOW] = (wide(above[:LOW]) + wide(got_up[:LOW])).astype(BF)
    to_up[LOW:HALF] = (
        wide(above[LOW:HALF]) + wide(got_up[LOW:HALF]) + wide(got_side[:cut])
    ).astype(BF)
    to_up[HALF:] = (wide(above[HALF:]) + wide(got_side[cut:HIGH])).astype(BF)
    to_down[:HALF] = (wide(below[:HALF]) + wide(got_side[HIGH : HIGH + HALF])).astype(BF)
    to_down[HALF:HIGH] = (
        wide(below[HALF:HIGH]) + wide(got_side[HIGH + HALF :]) + wide(got_down[:cut])
    ).astype(BF)
    to_down[HIGH:] = (wide(below[HIGH:]) + wide(got_down[cut:HALF])).astype(BF)
    to_side[:LOW] = (wide(beside[:LOW]) + wide(got_up[HALF:])).astype(BF)
    to_side[LOW:HIGH] = beside[LOW:HIGH]
    to_side[HIGH:] = (wide(beside[HIGH:]) + wide(got_down[HALF:])).astype(BF)


def both_hops_kernel(*refs):
    whole = 2 * HALF
    outs = refs[11:]
    third_hop_kernel(*refs[:6], *[ref.at[pl.ds(0, whole)] for ref in outs])
    second_hop_kernel(
        *refs[6:11], *[ref.at[pl.ds(whole, ref.shape[0] - whole)] for ref in outs]
    )


def last_kernel(own, from_below, from_above, from_side, total):
    rows = slice(0, 2 * HALF)
    total[...] = (
        (wide(own[...]) + wide(from_side[rows]))
        + (wide(from_below[rows]) + wide(from_above[rows]))
    ).astype(BF)


def final_hop_kernel(above, below, beside, got_up, got_down, got_side, to_up, to_down, to_side):
    got = [ref.at[pl.ds(2 * HALF, ref.shape[0] - 2 * HALF)] for ref in (got_up, got_down, got_side)]
    third_hop_kernel(above, below, beside, *got, to_up, to_down, to_side)


class Sums:
    def __init__(self, links):
        self.links = links

    def send(self, to_up, to_down, to_side):
        links = self.links
        return (links.send_up(to_up), links.send_down(to_down), links.cross(to_side))

    def first(self, sums):
        return (self.links.send_up(sums[0]), self.links.send_down(sums[1]))

    def second(self, *args):
        sizes = (HALF + LOW, HALF + LOW, 2 * HIGH)
        outgoing = local_call(second_hop_kernel, "second_hop", sizes, *args)
        return outgoing, self.send(*outgoing)

    def both(self, *args):
        sizes = (3 * HALF + LOW, 3 * HALF + LOW, 2 * HALF + 2 * HIGH)
        outgoing = local_call(both_hops_kernel, "both_hops", sizes, *args)
        return outgoing, self.send(*outgoing)

    def last(self, *args):
        outgoing = local_call(final_hop_kernel, "third_hop", (2 * HALF,) * 3, *args)
        return outgoing, self.send(*outgoing)

    def total(self, own, got):
        return local_call(last_kernel, "last_hop", (2 * HALF,), own, *got)[0]


def combine_kernel(pick_ref, gated_ref, out_ref, in_ref, mixed_ref, grads_ref):
    mixed_ref[...] = dot(gated_ref[...], wide(out_ref[...]), TN, lax.Precision.HIGHEST).astype(BF)
    grads_ref[...] = dot(pick_ref[...], in_ref[...], TN).astype(BF)


def combine(pick, gated, out_rows, in_rows):
    shape = jax.ShapeDtypeStruct((pick.shape[1], out_rows.shape[1]), BF)
    return pl.pallas_call(
        combine_kernel, out_shape=[shape] * 2, compiler_params=SMALL, name="combine"
    )(pick, gated, out_rows, in_rows)


def on_device(tokens, upstream, expert_ids, gate_values, gate_weight, up_weight, down_weight):
    columns = lax.axis_size("expert")
    exp_dev, hid, features = down_weight.shape
    rows = columns * exp_dev * 8
    width = tokens.shape[1]
    links = Links(lax.axis_size("dp"))
    order = block_order()
    columns_in = (in_hbm(gate_weight), in_hbm(up_weight))
    rows_in = in_hbm(down_weight.reshape(exp_dev * hid, features))

    def exchange(value):
        return lax.all_to_all(
            value.reshape(columns, exp_dev * 8, -1), "expert", 0, 0, tiled=True
        ).reshape(rows, -1)

    x_rows, c_rows, pick, gated = dispatch(expert_ids, gate_values, tokens, upstream, rows)
    arrived = exchange(jnp.concatenate([x_rows, c_rows], axis=1))
    x = Gather(links, arrived[:, :width])
    c = Gather(links, arrived[:, width:])
    x_sent = x.relay()
    pre = gate_up(0, order, after(x.arrived[0], *x_sent), columns_in)
    c_sent = c.relay(pre)
    total = cotangents(0, order, after(c.arrived[0], *c_sent), rows_in)
    x_sent = x.ends(total)
    pre = gate_up(1, order, after(x.arrived[1], *x_sent), columns_in, pre)
    c_sent = c.ends(pre)
    total = cotangents(1, order, after(c.arrived[1], *c_sent), rows_in, total)
    pre, hidden = gate_up(2, order, after(x.arrived[2], total), columns_in, pre)

    hops = Sums(links)
    out_cuts = output_sums(0, order, hidden, rows_in, width)
    out_got = hops.first(out_cuts)
    out_far = output_sums(1, order, after(hidden, *out_cuts, *c.arrived[2]), rows_in, width)
    diffs = cotangents(2, order, after(c.arrived[2], *out_far), rows_in, total, pre)
    sent, out_got = hops.second(*out_far, *after(out_got, *diffs))
    in_cuts = input_sums(0, order, after(diffs, *sent), columns_in, width)
    in_got = hops.first(in_cuts)
    in_far = input_sums(1, order, after(diffs, *in_cuts), columns_in, width)
    out_near = output_sums(2, order, after(hidden, *in_far), rows_in, width)
    sent, got = hops.both(*out_near[:3], *out_got, *in_far, *in_got)
    in_near = input_sums(2, order, after(diffs, *sent), columns_in, width)
    down_grad = row_grads(order, after(sum(c.arrived, ()), *in_near), hidden)
    gate_grad, up_grad = column_grads(order, after(sum(x.arrived, ()), down_grad), diffs)
    sent, in_got = hops.last(*in_near[:3], *after(got, gate_grad))
    out_back = exchange(hops.total(out_near[3], after(got, *sent)))
    in_back = exchange(hops.total(in_near[3], after(in_got, out_back)))
    mixed, token_grads = combine(pick, gated, out_back, in_back)
    return (mixed, token_grads, gate_grad, up_grad, down_grad.reshape(down_weight.shape))


def solution(mesh):
    return jax.shard_map(
        on_device,
        mesh=mesh,
        in_specs=(
            P("expert", "dp"),
            P("expert", "dp"),
            P("expert", None),
            P("expert", None),
            P("expert", None, "dp"),
            P("expert", None, "dp"),
            P("expert", "dp", None),
        ),
        out_specs=(
            P("expert", "dp"),
            P("expert", "dp"),
            P("expert", None, "dp"),
            P("expert", None, "dp"),
            P("expert", "dp", None),
        ),
        check_vma=False,
    )
```

```python
import jax
import jax.numpy as jnp
from jax import lax
from jax.experimental import pallas as pl
from jax.experimental.pallas import tpu as pltpu
from jax.sharding import PartitionSpec as P

BF = jnp.bfloat16
F32 = jnp.float32
HALF = 128
GATHER_LOW, OUT_LOW, IN_LOW = 112, 64, 112
ARRIVING = ((0, 1, 2, 3), (4, 5, 6), (7,))
LEAVING = ((7,), (4, 5, 6), (1, 2, 3, 0))
MIB = 1024 * 1024
SMALL = pltpu.CompilerParams(vmem_limit_bytes=8 * MIB)
LARGE = pltpu.CompilerParams(vmem_limit_bytes=16 * MIB)
HBM = pl.BlockSpec(memory_space=pl.ANY)
VMEM = pl.BlockSpec(memory_space=pltpu.VMEM)


def dot(a, b, dims=((1,), (0,)), precision=None):
    return lax.dot_general(a, b, (dims, ((), ())), precision=precision, preferred_element_type=F32)


def in_hbm(value):
    return pltpu.with_memory_space_constraint(value, pltpu.HBM)


class Copies:
    def __init__(self, semaphores):
        self.semaphores = semaphores
        self.used = 0

    def start(self, pairs):
        started = []
        for source, target in pairs:
            started.append(pltpu.make_async_copy(source, target, self.semaphores.at[self.used]))
            started[-1].start()
            self.used += 1
        return started


def wait(copies):
    for copy in copies:
        copy.wait()


def dispatch_kernel(
    ids_hbm, gates_hbm, tokens_ref, upstream_ref, x_ref, c_ref, pick_ref, gated_ref,
    ids_ref, gates_ref, held, semaphores,
):
    copies = Copies(semaphores)
    routes = copies.start(((ids_hbm, ids_ref), (gates_hbm, gates_ref)))
    arriving = copies.start(((tokens_ref, held.at[0]), (upstream_ref, held.at[1])))
    total, count = pick_ref.shape
    capacity = 8
    row = lax.broadcasted_iota(jnp.int32, (total, count), 0)
    expert = row // capacity
    wait(routes)
    named = jnp.zeros((total, count), F32)
    gate = jnp.zeros((total, count), F32)
    for k in range(ids_ref.shape[0]):
        hit = ids_ref[k : k + 1, :] == expert
        named = jnp.where(hit, 1.0, named)
        gate = jnp.where(hit, gates_ref[k : k + 1, :], gate)
    sooner = lax.broadcasted_iota(jnp.int32, (count, count), 0)
    later = lax.broadcasted_iota(jnp.int32, (count, count), 1)
    earlier = jnp.where(sooner < later, 1.0, 0.0)
    position = dot(named.astype(BF), earlier.astype(BF))
    chosen = (named > 0.5) & (position == (row % capacity).astype(F32))
    pick = jnp.where(chosen, 1.0, 0.0).astype(BF)
    gated = jnp.where(chosen, gate, 0.0)
    pick_ref[...] = pick
    gated_ref[...] = gated
    wait(arriving)
    x_ref[...] = dot(pick, held[0]).astype(BF)
    c_ref[...] = dot(gated, held[1].astype(F32), precision=lax.Precision.HIGHEST).astype(BF)


def dispatch(ids, gates, tokens, upstream, total):
    count, width = tokens.shape
    return pl.pallas_call(
        dispatch_kernel,
        in_specs=[HBM] * 4,
        out_shape=(
            jax.ShapeDtypeStruct((total, width), BF),
            jax.ShapeDtypeStruct((total, width), BF),
            jax.ShapeDtypeStruct((total, count), BF),
            jax.ShapeDtypeStruct((total, count), F32),
        ),
        scratch_shapes=[
            pltpu.VMEM((ids.shape[1], count), jnp.int32),
            pltpu.VMEM((ids.shape[1], count), F32),
            pltpu.VMEM((2, count, width), BF),
            pltpu.SemaphoreType.DMA((4,)),
        ],
        compiler_params=SMALL,
        name="dispatch",
    )(*[in_hbm(value) for value in (ids.T, gates.T, tokens, upstream)])


class Links:
    def __init__(self, size):
        rings = size // 2
        self.up = [(z * 2 + x, (z + 1) % rings * 2 + x) for z in range(rings) for x in range(2)]
        self.down = [(z * 2 + x, (z - 1) % rings * 2 + x) for z in range(rings) for x in range(2)]
        self.side = [(i, i ^ 1) for i in range(size)]

    def send_up(self, value):
        return lax.ppermute(value, "dp", self.up)

    def send_down(self, value):
        return lax.ppermute(value, "dp", self.down)

    def cross(self, value):
        return lax.ppermute(value, "dp", self.side)


def after(value, *earlier):
    return lax.optimization_barrier((value, *earlier))[0]


def local_call(kernel, name, sizes, *args):
    width = args[0].shape[1]
    shapes = tuple(jax.ShapeDtypeStruct((size, width), BF) for size in sizes)
    return pl.pallas_call(kernel, out_shape=shapes, compiler_params=SMALL, name=name)(*args)


def relay_kernel(above, below, beside, to_down, to_up, to_side):
    low, high = GATHER_LOW, 2 * HALF - GATHER_LOW
    to_down[:HALF] = above[:HALF]
    to_down[HALF:] = beside[:low]
    to_up[:HALF] = below[HALF:]
    to_up[HALF:] = beside[high:]
    to_side[:high] = above[low:]
    to_side[high:] = below[:high]


def ends_kernel(above2, below2, beside2, to_down, to_up):
    low, high = GATHER_LOW, 2 * HALF - GATHER_LOW
    to_down[:low] = above2[HALF:]
    to_down[low:] = beside2[: HALF - low]
    to_up[: HALF - low] = beside2[high + HALF :]
    to_up[HALF - low :] = below2[HALF:]


def hop_sizes(low):
    return (HALF + low, HALF + low, 2 * (2 * HALF - low))


class Gather:
    def __init__(self, links, own):
        self.links = links
        self.arrived = [(own, links.send_down(own), links.send_up(own), links.cross(own))]

    def relay(self, *earlier):
        links = self.links
        outgoing = local_call(
            relay_kernel,
            "relay",
            hop_sizes(GATHER_LOW),
            *after(self.arrived[0][1:], *earlier),
        )
        to_down, to_up, to_side = outgoing
        self.arrived.append(
            (links.send_down(to_down), links.send_up(to_up), links.cross(to_side))
        )
        return outgoing

    def ends(self, *earlier):
        links = self.links
        outgoing = local_call(ends_kernel, "ends", (HALF, HALF), *after(self.arrived[1], *earlier))
        self.arrived.append((links.send_down(outgoing[0]), links.send_up(outgoing[1])))
        return outgoing


def arrived_blocks(part, pieces):
    if part == 0:
        return [piece[...] for piece in pieces]
    stack = lambda a, b: jnp.concatenate([a, b], axis=0)
    if part == 1:
        above2, below2, beside2 = pieces
        high = 2 * HALF - GATHER_LOW
        return [
            stack(above2[:HALF], below2[:HALF]),
            stack(above2[HALF:], beside2[:high]),
            stack(beside2[high:], below2[HALF:]),
        ]
    return [stack(pieces[0][...], pieces[1][...])]


STEPS = ((0, 0), (1, 0), (-1, 0), (0, 1), (2, 0), (1, 1), (-1, 1), (2, 1))


def features_of(block, width):
    me = lax.axis_index("dp")
    rings = lax.axis_size("dp") // 2
    step_z, step_x = STEPS[block]
    z, x = me // 2, me % 2
    other = (z + step_z + rings) % rings * 2 + (x + step_x) % 2
    return pl.ds(pl.multiple_of(other * width, 128), width)


def row_slot(shape):
    return lax.broadcasted_iota(jnp.int32, shape, 0) // 8 % 2 == 0


def pair(first, value):
    zero = jnp.zeros_like(value)
    return jnp.concatenate([jnp.where(first, value, zero), jnp.where(first, zero, value)], axis=1)


def load_columns(copies, refs, buffers, blocks):
    width = buffers[0].shape[2]
    return [
        copies.start(
            [
                (ref.at[:, features_of(block, width), :], buffer.at[i])
                for ref, buffer in zip(refs, buffers)
            ]
        )
        for i, block in enumerate(blocks)
    ]


def load_rows(copies, ref, buffer, blocks):
    width = buffer.shape[2]
    return [
        copies.start([(ref.at[:, features_of(block, width)], buffer.at[i])])
        for i, block in enumerate(blocks)
    ]


def both(ref, i):
    return jnp.concatenate([ref[i, 0], ref[i, 1]], axis=1)


def column_buffers(blocks, width, hid):
    return [pltpu.VMEM((len(blocks), 2, width, hid), BF)] * 2


def row_buffers(blocks, width, hid):
    return [pltpu.VMEM((len(blocks), 2 * hid, width), BF)]


def semaphores_for(blocks, each):
    return [pltpu.SemaphoreType.DMA((each * len(blocks),))]


NT = ((1,), (1,))
TN = ((0,), (0,))


def gate_up(part, pieces, weights, before=None, down_flat=None):
    blocks = ARRIVING[part]
    rows, width = 2 * HALF, pieces[0].shape[1]
    hid = weights[0].shape[2]
    last = part == len(ARRIVING) - 1

    def kernel(*refs):
        count = len(pieces)
        held_pieces, refs = refs[:count], refs[count:]
        if before is not None:
            before_ref, refs = refs[0], refs[1:]
        columns, refs = refs[:2], refs[2:]
        if last:
            down_ref, pre_ref, hidden_ref, *cuts, gate_held, up_held, down_held, semaphores = refs
        else:
            pre_ref, gate_held, up_held, semaphores = refs
        copies = Copies(semaphores)
        arriving = load_columns(copies, columns, (gate_held, up_held), blocks)
        if last:
            down_arriving = load_rows(copies, down_ref, down_held, blocks)
        first = row_slot((rows, hid))
        for i, value in enumerate(arrived_blocks(part, held_pieces)):
            wait(arriving[i])
            gate = dot(value, both(gate_held, i))
            up = dot(value, both(up_held, i))
            gate = jnp.where(first, gate[:, :hid], gate[:, hid:])
            up = jnp.where(first, up[:, :hid], up[:, hid:])
            so_far = pre_ref if i else before_ref if before is not None else None
            if so_far is not None:
                gate += so_far[:, :hid]
                up += so_far[:, hid:]
            pre_ref[:, :hid] = gate
            pre_ref[:, hid:] = up
        if last:
            gate = pre_ref[:, :hid]
            hidden = pair(first, (gate * jax.nn.sigmoid(gate) * pre_ref[:, hid:]).astype(BF))
            hidden_ref[...] = hidden
            wait(down_arriving[0])
            store_sum(0, 0, dot(hidden, down_held[0]).astype(BF), cuts)

    shapes = [jax.ShapeDtypeStruct((rows, 2 * hid), F32)]
    scratch = column_buffers(blocks, width, hid)
    if last:
        shapes += [jax.ShapeDtypeStruct((rows, 2 * hid), BF)] + sum_shapes(0, rows, width)
        scratch += row_buffers(blocks, width, hid)
        weights = (*weights, down_flat)
    extra = [] if before is None else [before]
    out = pl.pallas_call(
        kernel,
        in_specs=[VMEM] * (len(pieces) + len(extra)) + [HBM] * len(weights),
        out_shape=shapes,
        scratch_shapes=scratch + semaphores_for(blocks, 3),
        compiler_params=LARGE,
        name=f"gate_up_{part}",
    )(*pieces, *extra, *weights)
    return out if last else out[0]


def output_sums(part, hidden, down_flat, width):
    blocks = LEAVING[part]
    rows, units = hidden.shape

    def kernel(hidden_ref, down_ref, *refs):
        outs = refs[:-2]
        down_held, semaphores = refs[-2:]
        arriving = load_rows(Copies(semaphores), down_ref, down_held, blocks)
        for i in range(len(blocks)):
            wait(arriving[i])
            store_sum(part, i, dot(hidden_ref[...], down_held[i]).astype(BF), outs)

    return pl.pallas_call(
        kernel,
        in_specs=[VMEM, HBM],
        out_shape=sum_shapes(part, rows, width),
        scratch_shapes=row_buffers(blocks, width, units // 2) + semaphores_for(blocks, 1),
        compiler_params=LARGE,
        name=f"output_sums_{part}",
    )(hidden, down_flat)


def sum_shapes(part, rows, width):
    sizes = (HALF, HALF) if part == 0 else (rows,) * len(LEAVING[part])
    return [jax.ShapeDtypeStruct((size, width), BF) for size in sizes]


def store_sum(part, i, value, outs):
    if part == 0:
        outs[0][...] = value[:HALF]
        outs[1][...] = value[HALF:]
    else:
        outs[i][...] = value


def cotangents(part, pieces, down_flat, before=None, pre=None, weights=()):
    blocks = ARRIVING[part]
    rows, width = 2 * HALF, pieces[0].shape[1]
    hid = down_flat.shape[0] // 2
    last = part == len(ARRIVING) - 1

    def kernel(*refs):
        count = len(pieces)
        held_pieces, refs = refs[:count], refs[count:]
        if before is not None:
            before_ref, refs = refs[0], refs[1:]
        if last:
            pre_ref, refs = refs[0], refs[1:]
        down_ref, refs = refs[0], refs[1:]
        if last:
            columns, refs = refs[:2], refs[2:]
            *outs, down_held, gate_held, up_held, semaphores = refs
        else:
            *outs, down_held, semaphores = refs
        copies = Copies(semaphores)
        arriving = load_rows(copies, down_ref, down_held, blocks)
        if last:
            columns_arriving = load_columns(copies, columns, (gate_held, up_held), blocks)
        first = row_slot((rows, hid))
        total = before_ref[...] if before is not None else None
        for i, value in enumerate(arrived_blocks(part, held_pieces)):
            wait(arriving[i])
            share = dot(value, down_held[i], NT)
            share = jnp.where(first, share[:, :hid], share[:, hid:])
            total = share if total is None else total + share
        if not last:
            outs[0][...] = total
            return
        gate, up = pre_ref[:, :hid], pre_ref[:, hid:]
        sigmoid = jax.nn.sigmoid(gate)
        gate_diff = (total * up * sigmoid * (1.0 + gate * (1.0 - sigmoid))).astype(BF)
        up_diff = (total * (gate * sigmoid)).astype(BF)
        gate_diff, up_diff = pair(first, gate_diff), pair(first, up_diff)
        outs[0][...] = gate_diff
        outs[1][...] = up_diff
        wait(columns_arriving[0])
        value = dot(gate_diff, both(gate_held, 0), NT) + dot(up_diff, both(up_held, 0), NT)
        store_sum(0, 0, value.astype(BF), outs[2:])

    scratch = row_buffers(blocks, width, hid)
    if last:
        shapes = [jax.ShapeDtypeStruct((rows, 2 * hid), BF)] * 2 + sum_shapes(0, rows, width)
        scratch += column_buffers(blocks, width, hid)
    else:
        shapes = [jax.ShapeDtypeStruct((rows, hid), F32)]
    extra = [value for value in (before, pre) if value is not None]
    out = pl.pallas_call(
        kernel,
        in_specs=[VMEM] * (len(pieces) + len(extra)) + [HBM] * (1 + len(weights)),
        out_shape=shapes,
        scratch_shapes=scratch + semaphores_for(blocks, 3),
        compiler_params=LARGE,
        name=f"cotangents_{part}",
    )(*pieces, *extra, down_flat, *weights)
    return out if last else out[0]


def input_sums(part, diffs, weights, width):
    blocks = LEAVING[part]
    rows, units = diffs[0].shape

    def kernel(gate_diff_ref, up_diff_ref, gate_ref, up_ref, *refs):
        outs = refs[:-3]
        gate_held, up_held, semaphores = refs[-3:]
        arriving = load_columns(
            Copies(semaphores), (gate_ref, up_ref), (gate_held, up_held), blocks
        )
        for i in range(len(blocks)):
            wait(arriving[i])
            value = dot(gate_diff_ref[...], both(gate_held, i), NT)
            value += dot(up_diff_ref[...], both(up_held, i), NT)
            store_sum(part, i, value.astype(BF), outs)

    return pl.pallas_call(
        kernel,
        in_specs=[VMEM, VMEM, HBM, HBM],
        out_shape=sum_shapes(part, rows, width),
        scratch_shapes=column_buffers(blocks, width, units // 2) + semaphores_for(blocks, 2),
        compiler_params=LARGE,
        name=f"input_sums_{part}",
    )(*diffs, *weights)


def middle_sums(diffs, hidden, weights, down_flat, width):
    in_blocks, out_blocks = LEAVING[1:]
    rows, units = hidden.shape

    def kernel(gate_diff_ref, up_diff_ref, hidden_ref, gate_ref, up_ref, down_ref, *refs):
        outs = refs[:-4]
        gate_held, up_held, down_held, semaphores = refs[-4:]
        copies = Copies(semaphores)
        arriving = load_columns(copies, (gate_ref, up_ref), (gate_held, up_held), in_blocks)
        down_arriving = load_rows(copies, down_ref, down_held, out_blocks)
        for i in range(len(in_blocks)):
            wait(arriving[i])
            value = dot(gate_diff_ref[...], both(gate_held, i), NT)
            value += dot(up_diff_ref[...], both(up_held, i), NT)
            outs[i][...] = value.astype(BF)
        for i in range(len(out_blocks)):
            wait(down_arriving[i])
            outs[len(in_blocks) + i][...] = dot(hidden_ref[...], down_held[i]).astype(BF)

    out = pl.pallas_call(
        kernel,
        in_specs=[VMEM] * 3 + [HBM] * 3,
        out_shape=sum_shapes(1, rows, width) + sum_shapes(2, rows, width),
        scratch_shapes=column_buffers(in_blocks, width, units // 2)
        + row_buffers(out_blocks, width, units // 2)
        + semaphores_for(range(10), 1),
        compiler_params=LARGE,
        name="middle_sums",
    )(*diffs, hidden, *weights, down_flat)
    return out[: len(in_blocks)], out[len(in_blocks) :]


def all_blocks(pieces):
    at = 0
    for part, count in enumerate((4, 3, 2)):
        for block, value in zip(ARRIVING[part], arrived_blocks(part, pieces[at : at + count])):
            yield block, value
        at += count


def column_grads_kernel(*refs):
    pieces = refs[:9]
    diffs, outs, held, semaphores = refs[9:11], refs[11:13], refs[13:15], refs[15]
    width, hid = held[0].shape[2:]
    copies = Copies(semaphores)
    leaving = []
    for block, value in all_blocks(pieces):
        for diff_ref, out_ref, held_ref in zip(diffs, outs, held):
            grad = dot(value, diff_ref[...], TN).astype(BF)
            held_ref[block, 0] = grad[:, :hid]
            held_ref[block, 1] = grad[:, hid:]
            target = out_ref.at[:, features_of(block, width), :]
            leaving += copies.start([(held_ref.at[block], target)])
    wait(leaving)


def column_grads(pieces, diffs):
    width = pieces[0].shape[1]
    hid = diffs[0].shape[1] // 2
    blocks = range(8)
    return pl.pallas_call(
        column_grads_kernel,
        in_specs=[VMEM] * 11,
        out_specs=[HBM] * 2,
        out_shape=[jax.ShapeDtypeStruct((2, 8 * width, hid), BF)] * 2,
        scratch_shapes=column_buffers(blocks, width, hid) + semaphores_for(blocks, 2),
        compiler_params=LARGE,
        name="column_grads",
    )(*pieces, *diffs)


def row_grads_kernel(*refs):
    pieces = refs[:9]
    hidden_ref, down_out, held, semaphores = refs[9:]
    width = held.shape[2]
    copies = Copies(semaphores)
    leaving = []
    for block, value in all_blocks(pieces):
        held[block] = dot(hidden_ref[...], value, TN).astype(BF)
        target = down_out.at[:, features_of(block, width)]
        leaving += copies.start([(held.at[block], target)])
    wait(leaving)


def row_grads(pieces, hidden):
    width = pieces[0].shape[1]
    units = hidden.shape[1]
    blocks = range(8)
    return pl.pallas_call(
        row_grads_kernel,
        in_specs=[VMEM] * 10,
        out_specs=HBM,
        out_shape=jax.ShapeDtypeStruct((units, 8 * width), BF),
        scratch_shapes=row_buffers(blocks, width, units // 2) + semaphores_for(blocks, 1),
        compiler_params=LARGE,
        name="row_grads",
    )(*pieces, hidden)


def wide(value):
    return value.astype(F32)


def second_hop(low, far, above1, below1, got_up, got_down, to_up, to_down, to_side):
    high, cut = 2 * HALF - low, HALF - low
    to_up[:HALF] = far[:HALF]
    to_up[HALF:] = (wide(above1[:low]) + wide(got_up[:low])).astype(BF)
    to_down[:HALF] = far[HALF:]
    to_down[HALF:] = (wide(below1[high:]) + wide(got_down[cut:])).astype(BF)
    to_side[:cut] = (wide(above1[low:HALF]) + wide(got_up[low:])).astype(BF)
    to_side[cut:high] = above1[HALF:]
    to_side[high : high + HALF] = below1[:HALF]
    to_side[high + HALF :] = (wide(below1[HALF:high]) + wide(got_down[:cut])).astype(BF)


def third_hop(low, above, below, beside, got_up, got_down, got_side, to_up, to_down, to_side):
    high, cut = 2 * HALF - low, HALF - low
    to_up[:low] = (wide(above[:low]) + wide(got_up[:low])).astype(BF)
    to_up[low:HALF] = (
        wide(above[low:HALF]) + wide(got_up[low:HALF]) + wide(got_side[:cut])
    ).astype(BF)
    to_up[HALF:] = (wide(above[HALF:]) + wide(got_side[cut:high])).astype(BF)
    to_down[:HALF] = (wide(below[:HALF]) + wide(got_side[high : high + HALF])).astype(BF)
    to_down[HALF:high] = (
        wide(below[HALF:high]) + wide(got_side[high + HALF :]) + wide(got_down[:cut])
    ).astype(BF)
    to_down[high:] = (wide(below[high:]) + wide(got_down[cut:HALF])).astype(BF)
    to_side[:low] = (wide(beside[:low]) + wide(got_up[HALF:])).astype(BF)
    to_side[low:high] = beside[low:high]
    to_side[high:] = (wide(beside[high:]) + wide(got_down[HALF:])).astype(BF)


def out_second_kernel(*refs):
    second_hop(OUT_LOW, *refs)


def both_hops_kernel(*refs):
    size = 2 * HALF
    outs = refs[11:]
    third_hop(OUT_LOW, *refs[:6], *[ref.at[pl.ds(0, size)] for ref in outs])
    second_hop(IN_LOW, *refs[6:11], *[ref.at[pl.ds(size, ref.shape[0] - size)] for ref in outs])


def in_third_kernel(above, below, beside, got_up, got_down, got_side, *outs):
    size = 2 * HALF
    got = [ref.at[pl.ds(size, ref.shape[0] - size)] for ref in (got_up, got_down, got_side)]
    third_hop(IN_LOW, above, below, beside, *got, *outs)


def last_kernel(own, from_below, from_above, from_side, total):
    rows = slice(0, 2 * HALF)
    total[...] = (
        (wide(own[...]) + wide(from_side[rows]))
        + (wide(from_below[rows]) + wide(from_above[rows]))
    ).astype(BF)


def final_hop_kernel(above, below, beside, got_up, got_down, got_side, to_up, to_down, to_side):
    got = [ref.at[pl.ds(2 * HALF, ref.shape[0] - 2 * HALF)] for ref in (got_up, got_down, got_side)]
    third_hop_kernel(above, below, beside, *got, to_up, to_down, to_side)


class Sums:
    def __init__(self, links):
        self.links = links

    def send(self, to_up, to_down, to_side):
        links = self.links
        return (links.send_up(to_up), links.send_down(to_down), links.cross(to_side))

    def first(self, sums):
        return (self.links.send_up(sums[0]), self.links.send_down(sums[1]))

    def second(self, *args):
        outgoing = local_call(out_second_kernel, "second_hop", hop_sizes(OUT_LOW), *args)
        return outgoing, self.send(*outgoing)

    def both(self, *args):
        sizes = tuple(2 * HALF + size for size in hop_sizes(IN_LOW))
        outgoing = local_call(both_hops_kernel, "both_hops", sizes, *args)
        return outgoing, self.send(*outgoing)

    def last(self, *args):
        outgoing = local_call(in_third_kernel, "third_hop", (2 * HALF,) * 3, *args)
        return outgoing, self.send(*outgoing)

    def total(self, own, got):
        return local_call(last_kernel, "last_hop", (2 * HALF,), own, *got)[0]


def combine_kernel(pick_ref, gated_ref, rows_ref, mixed_ref, grads_ref):
    width = mixed_ref.shape[1]
    mixed_ref[...] = dot(
        gated_ref[...], wide(rows_ref[:, :width]), TN, lax.Precision.HIGHEST
    ).astype(BF)
    grads_ref[...] = dot(pick_ref[...], rows_ref[:, width:], TN).astype(BF)


def combine(pick, gated, rows):
    shape = jax.ShapeDtypeStruct((pick.shape[1], rows.shape[1] // 2), BF)
    return pl.pallas_call(
        combine_kernel, out_shape=[shape] * 2, compiler_params=SMALL, name="combine"
    )(pick, gated, rows)


def on_device(tokens, upstream, expert_ids, gate_values, gate_weight, up_weight, down_weight):
    columns = lax.axis_size("expert")
    exp_dev, hid, features = down_weight.shape
    rows = columns * exp_dev * 8
    width = tokens.shape[1]
    links = Links(lax.axis_size("dp"))
    columns_in = (in_hbm(gate_weight), in_hbm(up_weight))
    rows_in = in_hbm(down_weight.reshape(exp_dev * hid, features))

    def exchange(value):
        return lax.all_to_all(
            value.reshape(columns, exp_dev * 8, -1), "expert", 0, 0, tiled=True
        ).reshape(rows, -1)

    x_rows, c_rows, pick, gated = dispatch(expert_ids, gate_values, tokens, upstream, rows)
    arrived = exchange(jnp.concatenate([x_rows, c_rows], axis=1))
    x = Gather(links, arrived[:, :width])
    c = Gather(links, arrived[:, width:])
    x_sent = x.relay()
    pre = gate_up(0, after(x.arrived[0], *x_sent), columns_in)
    c_sent = c.relay(pre)
    total = cotangents(0, after(c.arrived[0], *c_sent), rows_in)
    x_sent = x.ends(total)
    pre = gate_up(1, after(x.arrived[1], *x_sent), columns_in, pre)
    c_sent = c.ends(pre)
    total = cotangents(1, after(c.arrived[1], *c_sent), rows_in, total)
    pre, hidden, *out_cuts = gate_up(
        2, after(x.arrived[2], total), columns_in, pre, rows_in
    )

    hops = Sums(links)
    out_got = hops.first(out_cuts)
    out_far = output_sums(1, after(hidden, *out_cuts, *c.arrived[2]), rows_in, width)
    *diffs, cut_up, cut_down = cotangents(
        2, after(c.arrived[2], *out_far), rows_in, total, pre, columns_in
    )
    in_got = hops.first((cut_up, cut_down))
    sent, out_got = hops.second(*out_far, *after(out_got, cut_up))
    in_far, out_near = middle_sums(after(diffs, *sent), hidden, columns_in, rows_in, width)
    sent, got = hops.both(*out_near[:3], *out_got, *in_far, *in_got)
    in_near = input_sums(2, after(diffs, *sent), columns_in, width)
    down_grad = row_grads(after(sum(c.arrived, ()), *in_near), hidden)
    gate_grad, up_grad = column_grads(after(sum(x.arrived, ()), down_grad), diffs)
    sent, in_got = hops.last(*in_near[:3], *after(got, gate_grad))
    out_total = hops.total(out_near[3], after(got, *sent))
    in_total = hops.total(in_near[3], after(in_got, out_total))
    returned = exchange(jnp.concatenate([out_total, in_total], axis=1))
    mixed, token_grads = combine(pick, gated, returned)
    return (mixed, token_grads, gate_grad, up_grad, down_grad.reshape(down_weight.shape))


def solution(mesh):
    return jax.shard_map(
        on_device,
        mesh=mesh,
        in_specs=(
            P("expert", "dp"),
            P("expert", "dp"),
            P("expert", None),
            P("expert", None),
            P("expert", None, "dp"),
            P("expert", None, "dp"),
            P("expert", "dp", None),
        ),
        out_specs=(
            P("expert", "dp"),
            P("expert", "dp"),
            P("expert", None, "dp"),
            P("expert", None, "dp"),
            P("expert", "dp", None),
        ),
        check_vma=False,
    )
```

```python
import jax
import jax.numpy as jnp
from jax import lax
from jax.experimental import pallas as pl
from jax.experimental.pallas import tpu as pltpu
from jax.sharding import PartitionSpec as P

BF = jnp.bfloat16
F32 = jnp.float32
HALF = 128
GATHER_LOW, OUT_LOW, IN_LOW = 112, 80, 112
ARRIVING = ((0, 1, 2, 3), (4, 5, 6), (7,))
LEAVING = ((7,), (4, 5, 6), (1, 2, 3, 0))
MIB = 1024 * 1024
SMALL = pltpu.CompilerParams(vmem_limit_bytes=8 * MIB)
LARGE = pltpu.CompilerParams(vmem_limit_bytes=16 * MIB)
HBM = pl.BlockSpec(memory_space=pl.ANY)
VMEM = pl.BlockSpec(memory_space=pltpu.VMEM)


def dot(a, b, dims=((1,), (0,)), precision=None):
    return lax.dot_general(a, b, (dims, ((), ())), precision=precision, preferred_element_type=F32)


def in_hbm(value):
    return pltpu.with_memory_space_constraint(value, pltpu.HBM)


class Copies:
    def __init__(self, semaphores):
        self.semaphores = semaphores
        self.used = 0

    def start(self, pairs):
        started = []
        for source, target in pairs:
            started.append(pltpu.make_async_copy(source, target, self.semaphores.at[self.used]))
            started[-1].start()
            self.used += 1
        return started


def wait(copies):
    for copy in copies:
        copy.wait()


def exact_dot(weights, values, dims):
    high = weights.astype(BF)
    rest = weights - high.astype(F32)
    middle = rest.astype(BF)
    low = (rest - middle.astype(F32)).astype(BF)
    return (dot(low, values, dims) + dot(middle, values, dims)) + dot(high, values, dims)


def dispatch_kernel(
    ids_hbm, gates_hbm, tokens_ref, upstream_ref, x_ref, c_ref, pick_ref, gated_ref,
    ids_ref, gates_ref, held, semaphores,
):
    copies = Copies(semaphores)
    routes = copies.start(((ids_hbm, ids_ref), (gates_hbm, gates_ref)))
    arriving = copies.start(((tokens_ref, held.at[0]), (upstream_ref, held.at[1])))
    total, count = pick_ref.shape
    capacity = 8
    row = lax.broadcasted_iota(jnp.int32, (total, count), 0)
    expert = row // capacity
    wait(routes)
    named = jnp.zeros((total, count), F32)
    gate = jnp.zeros((total, count), F32)
    for k in range(ids_ref.shape[0]):
        hit = ids_ref[k : k + 1, :] == expert
        named = jnp.where(hit, 1.0, named)
        gate = jnp.where(hit, gates_ref[k : k + 1, :], gate)
    sooner = lax.broadcasted_iota(jnp.int32, (count, count), 0)
    later = lax.broadcasted_iota(jnp.int32, (count, count), 1)
    earlier = jnp.where(sooner < later, 1.0, 0.0)
    position = dot(named.astype(BF), earlier.astype(BF))
    chosen = (named > 0.5) & (position == (row % capacity).astype(F32))
    pick = jnp.where(chosen, 1.0, 0.0).astype(BF)
    gated = jnp.where(chosen, gate, 0.0)
    pick_ref[...] = pick
    gated_ref[...] = gated
    wait(arriving)
    x_ref[...] = dot(pick, held[0]).astype(BF)
    c_ref[...] = exact_dot(gated, held[1], ((1,), (0,))).astype(BF)


def dispatch(ids, gates, tokens, upstream, total):
    count, width = tokens.shape
    return pl.pallas_call(
        dispatch_kernel,
        in_specs=[HBM] * 4,
        out_shape=(
            jax.ShapeDtypeStruct((total, width), BF),
            jax.ShapeDtypeStruct((total, width), BF),
            jax.ShapeDtypeStruct((total, count), BF),
            jax.ShapeDtypeStruct((total, count), F32),
        ),
        scratch_shapes=[
            pltpu.VMEM((ids.shape[1], count), jnp.int32),
            pltpu.VMEM((ids.shape[1], count), F32),
            pltpu.VMEM((2, count, width), BF),
            pltpu.SemaphoreType.DMA((4,)),
        ],
        compiler_params=SMALL,
        name="dispatch",
    )(*[in_hbm(value) for value in (ids.T, gates.T, tokens, upstream)])


class Links:
    def __init__(self, size):
        rings = size // 2
        self.up = [(z * 2 + x, (z + 1) % rings * 2 + x) for z in range(rings) for x in range(2)]
        self.down = [(z * 2 + x, (z - 1) % rings * 2 + x) for z in range(rings) for x in range(2)]
        self.side = [(i, i ^ 1) for i in range(size)]

    def send_up(self, value):
        return lax.ppermute(value, "dp", self.up)

    def send_down(self, value):
        return lax.ppermute(value, "dp", self.down)

    def cross(self, value):
        return lax.ppermute(value, "dp", self.side)


def after(value, *earlier):
    return lax.optimization_barrier((value, *earlier))[0]


def local_call(kernel, name, sizes, *args):
    width = args[0].shape[1]
    shapes = tuple(jax.ShapeDtypeStruct((size, width), BF) for size in sizes)
    return pl.pallas_call(kernel, out_shape=shapes, compiler_params=SMALL, name=name)(*args)


def relay_kernel(above, below, beside, to_down, to_up, to_side):
    low, high = GATHER_LOW, 2 * HALF - GATHER_LOW
    to_down[:HALF] = above[:HALF]
    to_down[HALF:] = beside[:low]
    to_up[:HALF] = below[HALF:]
    to_up[HALF:] = beside[high:]
    to_side[:high] = above[low:]
    to_side[high:] = below[:high]


def ends_kernel(above2, below2, beside2, to_down, to_up):
    low, high = GATHER_LOW, 2 * HALF - GATHER_LOW
    to_down[:low] = above2[HALF:]
    to_down[low:] = beside2[: HALF - low]
    to_up[: HALF - low] = beside2[high + HALF :]
    to_up[HALF - low :] = below2[HALF:]


def hop_sizes(low):
    return (HALF + low, HALF + low, 2 * (2 * HALF - low))


class Gather:
    def __init__(self, links, own):
        self.links = links
        self.arrived = [(own, links.send_down(own), links.send_up(own), links.cross(own))]

    def relay(self, *earlier):
        links = self.links
        outgoing = local_call(
            relay_kernel,
            "relay",
            hop_sizes(GATHER_LOW),
            *after(self.arrived[0][1:], *earlier),
        )
        to_down, to_up, to_side = outgoing
        self.arrived.append(
            (links.send_down(to_down), links.send_up(to_up), links.cross(to_side))
        )
        return outgoing

    def ends(self, *earlier):
        links = self.links
        outgoing = local_call(ends_kernel, "ends", (HALF, HALF), *after(self.arrived[1], *earlier))
        self.arrived.append((links.send_down(outgoing[0]), links.send_up(outgoing[1])))
        return outgoing


def arrived_blocks(part, pieces):
    if part == 0:
        return [piece[...] for piece in pieces]
    stack = lambda a, b: jnp.concatenate([a, b], axis=0)
    if part == 1:
        above2, below2, beside2 = pieces
        high = 2 * HALF - GATHER_LOW
        return [
            stack(above2[:HALF], below2[:HALF]),
            stack(above2[HALF:], beside2[:high]),
            stack(beside2[high:], below2[HALF:]),
        ]
    return [stack(pieces[0][...], pieces[1][...])]


STEPS = ((0, 0), (1, 0), (-1, 0), (0, 1), (2, 0), (1, 1), (-1, 1), (2, 1))


def features_of(block, width):
    me = lax.axis_index("dp")
    rings = lax.axis_size("dp") // 2
    step_z, step_x = STEPS[block]
    z, x = me // 2, me % 2
    other = (z + step_z + rings) % rings * 2 + (x + step_x) % 2
    return pl.ds(pl.multiple_of(other * width, 128), width)


def row_slot(shape):
    return lax.broadcasted_iota(jnp.int32, shape, 0) // 8 % 2 == 0


def pair(first, value):
    zero = jnp.zeros_like(value)
    return jnp.concatenate([jnp.where(first, value, zero), jnp.where(first, zero, value)], axis=1)


def load_columns(copies, refs, buffers, blocks):
    width = buffers[0].shape[2]
    return [
        copies.start(
            [
                (ref.at[:, features_of(block, width), :], buffer.at[i])
                for ref, buffer in zip(refs, buffers)
            ]
        )
        for i, block in enumerate(blocks)
    ]


def load_rows(copies, ref, buffer, blocks):
    width = buffer.shape[2]
    return [
        copies.start([(ref.at[:, features_of(block, width)], buffer.at[i])])
        for i, block in enumerate(blocks)
    ]


def both(ref, i):
    return jnp.concatenate([ref[i, 0], ref[i, 1]], axis=1)


def column_buffers(blocks, width, hid):
    return [pltpu.VMEM((len(blocks), 2, width, hid), BF)] * 2


def row_buffers(blocks, width, hid):
    return [pltpu.VMEM((len(blocks), 2 * hid, width), BF)]


def semaphores_for(blocks, each):
    return [pltpu.SemaphoreType.DMA((each * len(blocks),))]


def fetch_kernel(gate_ref, up_ref, down_ref, gate_held, up_held, down_held, semaphores):
    copies = Copies(semaphores)
    arriving = load_columns(copies, (gate_ref, up_ref), (gate_held, up_held), ARRIVING[2])
    arriving += load_rows(copies, down_ref, down_held, ARRIVING[2])
    for started in arriving:
        wait(started)


def fetch_last(weights, down_flat, width):
    hid = weights[0].shape[2]
    columns = jax.ShapeDtypeStruct((1, 2, width, hid), BF)
    return pl.pallas_call(
        fetch_kernel,
        in_specs=[HBM] * 3,
        out_shape=(columns, columns, jax.ShapeDtypeStruct((1, 2 * hid, width), BF)),
        scratch_shapes=semaphores_for(range(3), 1),
        compiler_params=SMALL,
        name="fetch_last",
    )(*weights, down_flat)


NT = ((1,), (1,))
TN = ((0,), (0,))


def gate_up(part, pieces, weights, before=None, down_held=None):
    blocks = ARRIVING[part]
    rows, width = 2 * HALF, pieces[0].shape[1]
    hid = weights[0].shape[-1]
    last = part == len(ARRIVING) - 1

    def kernel(*refs):
        count = len(pieces)
        held_pieces, refs = refs[:count], refs[count:]
        if before is not None:
            before_ref, refs = refs[0], refs[1:]
        if last:
            gate_held, up_held, down_ref, pre_ref, hidden_ref, *cuts = refs
            arriving = [()]
        else:
            gate_ref, up_ref, pre_ref, gate_held, up_held, semaphores = refs
            arriving = load_columns(
                Copies(semaphores), (gate_ref, up_ref), (gate_held, up_held), blocks
            )
        first = row_slot((rows, hid))
        for i, value in enumerate(arrived_blocks(part, held_pieces)):
            wait(arriving[i])
            gate = dot(value, both(gate_held, i))
            up = dot(value, both(up_held, i))
            gate = jnp.where(first, gate[:, :hid], gate[:, hid:])
            up = jnp.where(first, up[:, :hid], up[:, hid:])
            so_far = pre_ref if i else before_ref if before is not None else None
            if so_far is not None:
                gate += so_far[:, :hid]
                up += so_far[:, hid:]
            pre_ref[:, :hid] = gate
            pre_ref[:, hid:] = up
        if last:
            gate = pre_ref[:, :hid]
            hidden = pair(first, (gate * jax.nn.sigmoid(gate) * pre_ref[:, hid:]).astype(BF))
            hidden_ref[...] = hidden
            store_sum(0, 0, dot(hidden, down_ref[0]).astype(BF), cuts)

    shapes = [jax.ShapeDtypeStruct((rows, 2 * hid), F32)]
    scratch = column_buffers(blocks, width, hid) + semaphores_for(blocks, 2)
    extra = [] if before is None else [before]
    if last:
        shapes += [jax.ShapeDtypeStruct((rows, 2 * hid), BF)] + sum_shapes(0, rows, width)
        scratch = []
        weights = (*weights, down_held)
    out = pl.pallas_call(
        kernel,
        in_specs=[VMEM] * (len(pieces) + len(extra)) + [VMEM if last else HBM] * len(weights),
        out_shape=shapes,
        scratch_shapes=scratch,
        compiler_params=LARGE,
        name=f"gate_up_{part}",
    )(*pieces, *extra, *weights)
    return out if last else out[0]


def output_sums(part, hidden, down_flat, width):
    blocks = LEAVING[part]
    rows, units = hidden.shape

    def kernel(hidden_ref, down_ref, *refs):
        outs = refs[:-2]
        down_held, semaphores = refs[-2:]
        arriving = load_rows(Copies(semaphores), down_ref, down_held, blocks)
        for i in range(len(blocks)):
            wait(arriving[i])
            store_sum(part, i, dot(hidden_ref[...], down_held[i]).astype(BF), outs)

    return pl.pallas_call(
        kernel,
        in_specs=[VMEM, HBM],
        out_shape=sum_shapes(part, rows, width),
        scratch_shapes=row_buffers(blocks, width, units // 2) + semaphores_for(blocks, 1),
        compiler_params=LARGE,
        name=f"output_sums_{part}",
    )(hidden, down_flat)


def sum_shapes(part, rows, width):
    sizes = (HALF, HALF) if part == 0 else (rows,) * len(LEAVING[part])
    return [jax.ShapeDtypeStruct((size, width), BF) for size in sizes]


def store_sum(part, i, value, outs):
    if part == 0:
        outs[0][...] = value[:HALF]
        outs[1][...] = value[HALF:]
    else:
        outs[i][...] = value


def cotangents(part, pieces, down_flat, before=None, pre=None, weights=()):
    blocks = ARRIVING[part]
    rows, width = 2 * HALF, pieces[0].shape[1]
    hid = down_flat.shape[-2] // 2
    last = part == len(ARRIVING) - 1

    def kernel(*refs):
        count = len(pieces)
        held_pieces, refs = refs[:count], refs[count:]
        if before is not None:
            before_ref, refs = refs[0], refs[1:]
        if last:
            pre_ref, down_held, gate_held, up_held, *outs = refs
            arriving = [()]
        else:
            down_ref, *outs, down_held, semaphores = refs
            arriving = load_rows(Copies(semaphores), down_ref, down_held, blocks)
        first = row_slot((rows, hid))
        total = before_ref[...] if before is not None else None
        for i, value in enumerate(arrived_blocks(part, held_pieces)):
            wait(arriving[i])
            share = dot(value, down_held[i], NT)
            share = jnp.where(first, share[:, :hid], share[:, hid:])
            total = share if total is None else total + share
        if not last:
            outs[0][...] = total
            return
        gate, up = pre_ref[:, :hid], pre_ref[:, hid:]
        sigmoid = jax.nn.sigmoid(gate)
        gate_diff = (total * up * sigmoid * (1.0 + gate * (1.0 - sigmoid))).astype(BF)
        up_diff = (total * (gate * sigmoid)).astype(BF)
        gate_diff, up_diff = pair(first, gate_diff), pair(first, up_diff)
        outs[0][...] = gate_diff
        outs[1][...] = up_diff
        value = dot(gate_diff, both(gate_held, 0), NT) + dot(up_diff, both(up_held, 0), NT)
        store_sum(0, 0, value.astype(BF), outs[2:])

    if last:
        shapes = [jax.ShapeDtypeStruct((rows, 2 * hid), BF)] * 2 + sum_shapes(0, rows, width)
        scratch = []
    else:
        shapes = [jax.ShapeDtypeStruct((rows, hid), F32)]
        scratch = row_buffers(blocks, width, hid) + semaphores_for(blocks, 1)
    extra = [value for value in (before, pre) if value is not None]
    held = [VMEM if last else HBM] * (1 + len(weights))
    out = pl.pallas_call(
        kernel,
        in_specs=[VMEM] * (len(pieces) + len(extra)) + held,
        out_shape=shapes,
        scratch_shapes=scratch,
        compiler_params=LARGE,
        name=f"cotangents_{part}",
    )(*pieces, *extra, down_flat, *weights)
    return out if last else out[0]


def input_sums(part, diffs, weights, width):
    blocks = LEAVING[part]
    rows, units = diffs[0].shape

    def kernel(gate_diff_ref, up_diff_ref, gate_ref, up_ref, *refs):
        outs = refs[:-3]
        gate_held, up_held, semaphores = refs[-3:]
        arriving = load_columns(
            Copies(semaphores), (gate_ref, up_ref), (gate_held, up_held), blocks
        )
        for i in range(len(blocks)):
            wait(arriving[i])
            value = dot(gate_diff_ref[...], both(gate_held, i), NT)
            value += dot(up_diff_ref[...], both(up_held, i), NT)
            store_sum(part, i, value.astype(BF), outs)

    return pl.pallas_call(
        kernel,
        in_specs=[VMEM, VMEM, HBM, HBM],
        out_shape=sum_shapes(part, rows, width),
        scratch_shapes=column_buffers(blocks, width, units // 2) + semaphores_for(blocks, 2),
        compiler_params=LARGE,
        name=f"input_sums_{part}",
    )(*diffs, *weights)


def middle_sums(diffs, hidden, weights, down_flat, width):
    in_blocks, out_blocks = LEAVING[1:]
    rows, units = hidden.shape

    def kernel(gate_diff_ref, up_diff_ref, hidden_ref, gate_ref, up_ref, down_ref, *refs):
        outs = refs[:-4]
        gate_held, up_held, down_held, semaphores = refs[-4:]
        copies = Copies(semaphores)
        arriving = load_columns(copies, (gate_ref, up_ref), (gate_held, up_held), in_blocks)
        down_arriving = load_rows(copies, down_ref, down_held, out_blocks)
        for i in range(len(in_blocks)):
            wait(arriving[i])
            value = dot(gate_diff_ref[...], both(gate_held, i), NT)
            value += dot(up_diff_ref[...], both(up_held, i), NT)
            outs[i][...] = value.astype(BF)
        for i in range(len(out_blocks)):
            wait(down_arriving[i])
            outs[len(in_blocks) + i][...] = dot(hidden_ref[...], down_held[i]).astype(BF)

    out = pl.pallas_call(
        kernel,
        in_specs=[VMEM] * 3 + [HBM] * 3,
        out_shape=sum_shapes(1, rows, width) + sum_shapes(2, rows, width),
        scratch_shapes=column_buffers(in_blocks, width, units // 2)
        + row_buffers(out_blocks, width, units // 2)
        + semaphores_for(range(10), 1),
        compiler_params=LARGE,
        name="middle_sums",
    )(*diffs, hidden, *weights, down_flat)
    return out[: len(in_blocks)], out[len(in_blocks) :]


def all_blocks(pieces):
    at = 0
    for part, count in enumerate((4, 3, 2)):
        for block, value in zip(ARRIVING[part], arrived_blocks(part, pieces[at : at + count])):
            yield block, value
        at += count


def column_grads_kernel(*refs):
    pieces = refs[:9]
    diffs, outs, held, semaphores = refs[9:11], refs[11:13], refs[13:15], refs[15]
    width, hid = held[0].shape[2:]
    copies = Copies(semaphores)
    leaving = []
    for block, value in all_blocks(pieces):
        for diff_ref, out_ref, held_ref in zip(diffs, outs, held):
            grad = dot(value, diff_ref[...], TN).astype(BF)
            held_ref[block, 0] = grad[:, :hid]
            held_ref[block, 1] = grad[:, hid:]
            target = out_ref.at[:, features_of(block, width), :]
            leaving += copies.start([(held_ref.at[block], target)])
    wait(leaving)


def column_grads(pieces, diffs):
    width = pieces[0].shape[1]
    hid = diffs[0].shape[1] // 2
    blocks = range(8)
    return pl.pallas_call(
        column_grads_kernel,
        in_specs=[VMEM] * 11,
        out_specs=[HBM] * 2,
        out_shape=[jax.ShapeDtypeStruct((2, 8 * width, hid), BF)] * 2,
        scratch_shapes=column_buffers(blocks, width, hid) + semaphores_for(blocks, 2),
        compiler_params=LARGE,
        name="column_grads",
    )(*pieces, *diffs)


def row_grads_kernel(*refs):
    pieces = refs[:9]
    hidden_ref, down_out, held, semaphores = refs[9:]
    width = held.shape[2]
    copies = Copies(semaphores)
    leaving = []
    for block, value in all_blocks(pieces):
        held[block] = dot(hidden_ref[...], value, TN).astype(BF)
        target = down_out.at[:, features_of(block, width)]
        leaving += copies.start([(held.at[block], target)])
    wait(leaving)


def row_grads(pieces, hidden):
    width = pieces[0].shape[1]
    units = hidden.shape[1]
    blocks = range(8)
    return pl.pallas_call(
        row_grads_kernel,
        in_specs=[VMEM] * 10,
        out_specs=HBM,
        out_shape=jax.ShapeDtypeStruct((units, 8 * width), BF),
        scratch_shapes=row_buffers(blocks, width, units // 2) + semaphores_for(blocks, 1),
        compiler_params=LARGE,
        name="row_grads",
    )(*pieces, hidden)


def wide(value):
    return value.astype(F32)


def second_hop(low, far, above1, below1, got_up, got_down, to_up, to_down, to_side):
    high, cut = 2 * HALF - low, HALF - low
    to_up[:HALF] = far[:HALF]
    to_up[HALF:] = (wide(above1[:low]) + wide(got_up[:low])).astype(BF)
    to_down[:HALF] = far[HALF:]
    to_down[HALF:] = (wide(below1[high:]) + wide(got_down[cut:])).astype(BF)
    to_side[:cut] = (wide(above1[low:HALF]) + wide(got_up[low:])).astype(BF)
    to_side[cut:high] = above1[HALF:]
    to_side[high : high + HALF] = below1[:HALF]
    to_side[high + HALF :] = (wide(below1[HALF:high]) + wide(got_down[:cut])).astype(BF)


def third_hop(low, above, below, beside, got_up, got_down, got_side, to_up, to_down, to_side):
    high, cut = 2 * HALF - low, HALF - low
    to_up[:low] = (wide(above[:low]) + wide(got_up[:low])).astype(BF)
    to_up[low:HALF] = (
        wide(above[low:HALF]) + wide(got_up[low:HALF]) + wide(got_side[:cut])
    ).astype(BF)
    to_up[HALF:] = (wide(above[HALF:]) + wide(got_side[cut:high])).astype(BF)
    to_down[:HALF] = (wide(below[:HALF]) + wide(got_side[high : high + HALF])).astype(BF)
    to_down[HALF:high] = (
        wide(below[HALF:high]) + wide(got_side[high + HALF :]) + wide(got_down[:cut])
    ).astype(BF)
    to_down[high:] = (wide(below[high:]) + wide(got_down[cut:HALF])).astype(BF)
    to_side[:low] = (wide(beside[:low]) + wide(got_up[HALF:])).astype(BF)
    to_side[low:high] = beside[low:high]
    to_side[high:] = (wide(beside[high:]) + wide(got_down[HALF:])).astype(BF)


def out_second_kernel(*refs):
    second_hop(OUT_LOW, *refs)


def both_hops_kernel(*refs):
    size = 2 * HALF
    outs = refs[11:]
    third_hop(OUT_LOW, *refs[:6], *[ref.at[pl.ds(0, size)] for ref in outs])
    second_hop(IN_LOW, *refs[6:11], *[ref.at[pl.ds(size, ref.shape[0] - size)] for ref in outs])


def in_third_kernel(above, below, beside, got_up, got_down, got_side, *outs):
    size = 2 * HALF
    got = [ref.at[pl.ds(size, ref.shape[0] - size)] for ref in (got_up, got_down, got_side)]
    third_hop(IN_LOW, above, below, beside, *got, *outs)


def last_kernel(own, from_below, from_above, from_side, total):
    rows = slice(0, 2 * HALF)
    total[...] = (
        (wide(own[...]) + wide(from_side[rows]))
        + (wide(from_below[rows]) + wide(from_above[rows]))
    ).astype(BF)


def final_hop_kernel(above, below, beside, got_up, got_down, got_side, to_up, to_down, to_side):
    got = [ref.at[pl.ds(2 * HALF, ref.shape[0] - 2 * HALF)] for ref in (got_up, got_down, got_side)]
    third_hop_kernel(above, below, beside, *got, to_up, to_down, to_side)


class Sums:
    def __init__(self, links):
        self.links = links

    def send(self, to_up, to_down, to_side):
        links = self.links
        return (links.send_up(to_up), links.send_down(to_down), links.cross(to_side))

    def first(self, sums):
        return (self.links.send_up(sums[0]), self.links.send_down(sums[1]))

    def second(self, *args):
        outgoing = local_call(out_second_kernel, "second_hop", hop_sizes(OUT_LOW), *args)
        return outgoing, self.send(*outgoing)

    def both(self, *args):
        sizes = tuple(2 * HALF + size for size in hop_sizes(IN_LOW))
        outgoing = local_call(both_hops_kernel, "both_hops", sizes, *args)
        return outgoing, self.send(*outgoing)

    def last(self, *args):
        outgoing = local_call(in_third_kernel, "third_hop", (2 * HALF,) * 3, *args)
        return outgoing, self.send(*outgoing)

    def total(self, own, got):
        return local_call(last_kernel, "last_hop", (2 * HALF,), own, *got)[0]


def combine_kernel(pick_ref, gated_ref, rows_ref, mixed_ref, grads_ref):
    width = mixed_ref.shape[1]
    mixed_ref[...] = exact_dot(gated_ref[...], rows_ref[:, :width], TN).astype(BF)
    grads_ref[...] = dot(pick_ref[...], rows_ref[:, width:], TN).astype(BF)


def combine(pick, gated, rows):
    shape = jax.ShapeDtypeStruct((pick.shape[1], rows.shape[1] // 2), BF)
    return pl.pallas_call(
        combine_kernel, out_shape=[shape] * 2, compiler_params=SMALL, name="combine"
    )(pick, gated, rows)


def on_device(tokens, upstream, expert_ids, gate_values, gate_weight, up_weight, down_weight):
    columns = lax.axis_size("expert")
    exp_dev, hid, features = down_weight.shape
    rows = columns * exp_dev * 8
    width = tokens.shape[1]
    links = Links(lax.axis_size("dp"))
    columns_in = (in_hbm(gate_weight), in_hbm(up_weight))
    rows_in = in_hbm(down_weight.reshape(exp_dev * hid, features))

    def exchange(value):
        return lax.all_to_all(
            value.reshape(columns, exp_dev * 8, -1), "expert", 0, 0, tiled=True
        ).reshape(rows, -1)

    x_rows, c_rows, pick, gated = dispatch(expert_ids, gate_values, tokens, upstream, rows)
    arrived = exchange(jnp.concatenate([x_rows, c_rows], axis=1))
    x = Gather(links, arrived[:, :width])
    c = Gather(links, arrived[:, width:])
    x_sent = x.relay()
    pre = gate_up(0, after(x.arrived[0], *x_sent), columns_in)
    *last_columns, last_rows = fetch_last(after(columns_in, pre), rows_in, width)
    c_sent = c.relay(pre, last_rows)
    total = cotangents(0, after(c.arrived[0], *c_sent), rows_in)
    x_sent = x.ends(total)
    pre = gate_up(1, after(x.arrived[1], *x_sent), columns_in, pre)
    c_sent = c.ends(pre)
    total = cotangents(1, after(c.arrived[1], *c_sent), rows_in, total)
    pre, hidden, *out_cuts = gate_up(
        2, after(x.arrived[2], total), last_columns, pre, last_rows
    )

    hops = Sums(links)
    out_got = hops.first(out_cuts)
    out_far = output_sums(1, after(hidden, *out_cuts), rows_in, width)
    *diffs, cut_up, cut_down = cotangents(
        2, after(c.arrived[2], *out_far), last_rows, total, pre, last_columns
    )
    in_got = hops.first((cut_up, cut_down))
    sent, out_got = hops.second(*out_far, *after(out_got, cut_up))
    in_far, out_near = middle_sums(after(diffs, *sent), hidden, columns_in, rows_in, width)
    sent, got = hops.both(*out_near[:3], *out_got, *in_far, *in_got)
    in_near = input_sums(2, after(diffs, *sent), columns_in, width)
    down_grad = row_grads(after(sum(c.arrived, ()), *in_near), hidden)
    gate_grad, up_grad = column_grads(after(sum(x.arrived, ()), down_grad), diffs)
    sent, in_got = hops.last(*in_near[:3], *after(got, gate_grad))
    out_total = hops.total(out_near[3], after(got, *sent))
    in_total = hops.total(in_near[3], after(in_got, out_total))
    returned = exchange(jnp.concatenate([out_total, in_total], axis=1))
    mixed, token_grads = combine(pick, gated, returned)
    return (mixed, token_grads, gate_grad, up_grad, down_grad.reshape(down_weight.shape))


def solution(mesh):
    return jax.shard_map(
        on_device,
        mesh=mesh,
        in_specs=(
            P("expert", "dp"),
            P("expert", "dp"),
            P("expert", None),
            P("expert", None),
            P("expert", None, "dp"),
            P("expert", None, "dp"),
            P("expert", "dp", None),
        ),
        out_specs=(
            P("expert", "dp"),
            P("expert", "dp"),
            P("expert", None, "dp"),
            P("expert", None, "dp"),
            P("expert", "dp", None),
        ),
        check_vma=False,
    )
```

```python
import jax
import jax.numpy as jnp
from jax import lax
from jax.experimental import pallas as pl
from jax.experimental.pallas import tpu as pltpu
from jax.sharding import PartitionSpec as P

BF = jnp.bfloat16
F32 = jnp.float32
HALF = 128
GATHER_LOW, OUT_LOW, IN_LOW = 112, 80, 112
ARRIVING = ((0, 1, 2, 3), (4, 5, 6), (7,))
LEAVING = ((7,), (4, 5, 6), (1, 2, 3, 0))
MIB = 1024 * 1024
SMALL = pltpu.CompilerParams(vmem_limit_bytes=8 * MIB)
LARGE = pltpu.CompilerParams(vmem_limit_bytes=16 * MIB)
HBM = pl.BlockSpec(memory_space=pl.ANY)
VMEM = pl.BlockSpec(memory_space=pltpu.VMEM)


def dot(a, b, dims=((1,), (0,)), precision=None):
    return lax.dot_general(a, b, (dims, ((), ())), precision=precision, preferred_element_type=F32)


def in_hbm(value):
    return pltpu.with_memory_space_constraint(value, pltpu.HBM)


class Copies:
    def __init__(self, semaphores):
        self.semaphores = semaphores
        self.used = 0

    def start(self, pairs):
        started = []
        for source, target in pairs:
            started.append(pltpu.make_async_copy(source, target, self.semaphores.at[self.used]))
            started[-1].start()
            self.used += 1
        return started


def wait(copies):
    for copy in copies:
        copy.wait()


def exact_dot(weights, values, dims):
    high = weights.astype(BF)
    rest = weights - high.astype(F32)
    middle = rest.astype(BF)
    low = (rest - middle.astype(F32)).astype(BF)
    return (dot(low, values, dims) + dot(middle, values, dims)) + dot(high, values, dims)


def dispatch_kernel(
    ids_hbm, gates_hbm, tokens_ref, upstream_ref, x_ref, c_ref, pick_ref, gated_ref,
    ids_ref, gates_ref, held, semaphores,
):
    copies = Copies(semaphores)
    routes = copies.start(((ids_hbm, ids_ref), (gates_hbm, gates_ref)))
    arriving = copies.start(((tokens_ref, held.at[0]), (upstream_ref, held.at[1])))
    total, count = pick_ref.shape
    capacity = 8
    row = lax.broadcasted_iota(jnp.int32, (total, count), 0)
    expert = row // capacity
    wait(routes)
    named = jnp.zeros((total, count), F32)
    gate = jnp.zeros((total, count), F32)
    for k in range(ids_ref.shape[0]):
        hit = ids_ref[k : k + 1, :] == expert
        named = jnp.where(hit, 1.0, named)
        gate = jnp.where(hit, gates_ref[k : k + 1, :], gate)
    sooner = lax.broadcasted_iota(jnp.int32, (count, count), 0)
    later = lax.broadcasted_iota(jnp.int32, (count, count), 1)
    earlier = jnp.where(sooner < later, 1.0, 0.0)
    position = dot(named.astype(BF), earlier.astype(BF))
    chosen = (named > 0.5) & (position == (row % capacity).astype(F32))
    pick = jnp.where(chosen, 1.0, 0.0).astype(BF)
    gated = jnp.where(chosen, gate, 0.0)
    pick_ref[...] = pick
    gated_ref[...] = gated
    wait(arriving)
    x_ref[...] = dot(pick, held[0]).astype(BF)
    c_ref[...] = exact_dot(gated, held[1], ((1,), (0,))).astype(BF)


def dispatch(ids, gates, tokens, upstream, total):
    count, width = tokens.shape
    return pl.pallas_call(
        dispatch_kernel,
        in_specs=[HBM] * 4,
        out_shape=(
            jax.ShapeDtypeStruct((total, width), BF),
            jax.ShapeDtypeStruct((total, width), BF),
            jax.ShapeDtypeStruct((total, count), BF),
            jax.ShapeDtypeStruct((total, count), F32),
        ),
        scratch_shapes=[
            pltpu.VMEM((ids.shape[1], count), jnp.int32),
            pltpu.VMEM((ids.shape[1], count), F32),
            pltpu.VMEM((2, count, width), BF),
            pltpu.SemaphoreType.DMA((4,)),
        ],
        compiler_params=SMALL,
        name="dispatch",
    )(*[in_hbm(value) for value in (ids.T, gates.T, tokens, upstream)])


class Links:
    def __init__(self, size):
        rings = size // 2
        self.up = [(z * 2 + x, (z + 1) % rings * 2 + x) for z in range(rings) for x in range(2)]
        self.down = [(z * 2 + x, (z - 1) % rings * 2 + x) for z in range(rings) for x in range(2)]
        self.side = [(i, i ^ 1) for i in range(size)]

    def send_up(self, value):
        return lax.ppermute(value, "dp", self.up)

    def send_down(self, value):
        return lax.ppermute(value, "dp", self.down)

    def cross(self, value):
        return lax.ppermute(value, "dp", self.side)


def after(value, *earlier):
    return lax.optimization_barrier((value, *earlier))[0]


def local_call(kernel, name, sizes, *args):
    width = args[0].shape[1]
    shapes = tuple(jax.ShapeDtypeStruct((size, width), BF) for size in sizes)
    return pl.pallas_call(kernel, out_shape=shapes, compiler_params=SMALL, name=name)(*args)


def relay_kernel(above, below, beside, to_down, to_up, to_side):
    low, high = GATHER_LOW, 2 * HALF - GATHER_LOW
    to_down[:HALF] = above[:HALF]
    to_down[HALF:] = beside[:low]
    to_up[:HALF] = below[HALF:]
    to_up[HALF:] = beside[high:]
    to_side[:high] = above[low:]
    to_side[high:] = below[:high]


def ends_kernel(above2, below2, beside2, to_down, to_up):
    low, high = GATHER_LOW, 2 * HALF - GATHER_LOW
    to_down[:low] = above2[HALF:]
    to_down[low:] = beside2[: HALF - low]
    to_up[: HALF - low] = beside2[high + HALF :]
    to_up[HALF - low :] = below2[HALF:]


def hop_sizes(low):
    return (HALF + low, HALF + low, 2 * (2 * HALF - low))


class Gather:
    def __init__(self, links, own):
        self.links = links
        self.arrived = [(own, links.send_down(own), links.send_up(own), links.cross(own))]

    def relay(self, *earlier):
        links = self.links
        outgoing = local_call(
            relay_kernel,
            "relay",
            hop_sizes(GATHER_LOW),
            *after(self.arrived[0][1:], *earlier),
        )
        to_down, to_up, to_side = outgoing
        self.arrived.append(
            (links.send_down(to_down), links.send_up(to_up), links.cross(to_side))
        )
        return outgoing

    def ends(self, *earlier):
        links = self.links
        outgoing = local_call(ends_kernel, "ends", (HALF, HALF), *after(self.arrived[1], *earlier))
        self.arrived.append((links.send_down(outgoing[0]), links.send_up(outgoing[1])))
        return outgoing


def arrived_blocks(part, pieces):
    if part == 0:
        return [piece[...] for piece in pieces]
    stack = lambda a, b: jnp.concatenate([a, b], axis=0)
    if part == 1:
        above2, below2, beside2 = pieces
        high = 2 * HALF - GATHER_LOW
        return [
            stack(above2[:HALF], below2[:HALF]),
            stack(above2[HALF:], beside2[:high]),
            stack(beside2[high:], below2[HALF:]),
        ]
    return [stack(pieces[0][...], pieces[1][...])]


STEPS = ((0, 0), (1, 0), (-1, 0), (0, 1), (2, 0), (1, 1), (-1, 1), (2, 1))


def features_of(block, width):
    me = lax.axis_index("dp")
    rings = lax.axis_size("dp") // 2
    step_z, step_x = STEPS[block]
    z, x = me // 2, me % 2
    other = (z + step_z + rings) % rings * 2 + (x + step_x) % 2
    return pl.ds(pl.multiple_of(other * width, 128), width)


def row_slot(shape):
    return lax.broadcasted_iota(jnp.int32, shape, 0) // 8 % 2 == 0


def pair(first, value):
    zero = jnp.zeros_like(value)
    return jnp.concatenate([jnp.where(first, value, zero), jnp.where(first, zero, value)], axis=1)


def load_columns(copies, refs, buffers, blocks):
    width = buffers[0].shape[2]
    return [
        copies.start(
            [
                (ref.at[:, features_of(block, width), :], buffer.at[i])
                for ref, buffer in zip(refs, buffers)
            ]
        )
        for i, block in enumerate(blocks)
    ]


def load_rows(copies, ref, buffer, blocks):
    width = buffer.shape[2]
    return [
        copies.start([(ref.at[:, features_of(block, width)], buffer.at[i])])
        for i, block in enumerate(blocks)
    ]


def both(ref, i):
    return jnp.concatenate([ref[i, 0], ref[i, 1]], axis=1)


def column_buffers(blocks, width, hid):
    return [pltpu.VMEM((len(blocks), 2, width, hid), BF)] * 2


def row_buffers(blocks, width, hid):
    return [pltpu.VMEM((len(blocks), 2 * hid, width), BF)]


def semaphores_for(blocks, each):
    return [pltpu.SemaphoreType.DMA((each * len(blocks),))]


def fetch_kernel(gate_ref, up_ref, down_ref, gate_held, up_held, down_held, semaphores):
    copies = Copies(semaphores)
    arriving = load_columns(copies, (gate_ref, up_ref), (gate_held, up_held), ARRIVING[2])
    arriving += load_rows(copies, down_ref, down_held, ARRIVING[2])
    for started in arriving:
        wait(started)


def fetch_last(weights, down_flat, width):
    hid = weights[0].shape[2]
    columns = jax.ShapeDtypeStruct((1, 2, width, hid), BF)
    return pl.pallas_call(
        fetch_kernel,
        in_specs=[HBM] * 3,
        out_shape=(columns, columns, jax.ShapeDtypeStruct((1, 2 * hid, width), BF)),
        scratch_shapes=semaphores_for(range(3), 1),
        compiler_params=SMALL,
        name="fetch_last",
    )(*weights, down_flat)


NT = ((1,), (1,))
TN = ((0,), (0,))


def gate_up(part, pieces, weights, before=None, down_held=None):
    blocks = ARRIVING[part]
    rows, width = 2 * HALF, pieces[0].shape[1]
    hid = weights[0].shape[-1]
    last = part == len(ARRIVING) - 1

    def kernel(*refs):
        count = len(pieces)
        held_pieces, refs = refs[:count], refs[count:]
        if before is not None:
            before_ref, refs = refs[0], refs[1:]
        if last:
            gate_held, up_held, down_ref, pre_ref, hidden_ref, *cuts = refs
            arriving = [()]
        else:
            gate_ref, up_ref, pre_ref, gate_held, up_held, semaphores = refs
            arriving = load_columns(
                Copies(semaphores), (gate_ref, up_ref), (gate_held, up_held), blocks
            )
        first = row_slot((rows, hid))
        for i, value in enumerate(arrived_blocks(part, held_pieces)):
            wait(arriving[i])
            gate = dot(value, both(gate_held, i))
            up = dot(value, both(up_held, i))
            gate = jnp.where(first, gate[:, :hid], gate[:, hid:])
            up = jnp.where(first, up[:, :hid], up[:, hid:])
            so_far = pre_ref if i else before_ref if before is not None else None
            if so_far is not None:
                gate += so_far[:, :hid]
                up += so_far[:, hid:]
            pre_ref[:, :hid] = gate
            pre_ref[:, hid:] = up
        if last:
            gate = pre_ref[:, :hid]
            hidden = pair(first, (gate * jax.nn.sigmoid(gate) * pre_ref[:, hid:]).astype(BF))
            hidden_ref[...] = hidden
            store_sum(0, 0, dot(hidden, down_ref[0]).astype(BF), cuts)

    shapes = [jax.ShapeDtypeStruct((rows, 2 * hid), F32)]
    scratch = column_buffers(blocks, width, hid) + semaphores_for(blocks, 2)
    extra = [] if before is None else [before]
    if last:
        shapes += [jax.ShapeDtypeStruct((rows, 2 * hid), BF)] + sum_shapes(0, rows, width)
        scratch = []
        weights = (*weights, down_held)
    out = pl.pallas_call(
        kernel,
        in_specs=[VMEM] * (len(pieces) + len(extra)) + [VMEM if last else HBM] * len(weights),
        out_shape=shapes,
        scratch_shapes=scratch,
        compiler_params=LARGE,
        name=f"gate_up_{part}",
    )(*pieces, *extra, *weights)
    return out if last else out[0]


def output_sums(part, hidden, down_flat, width):
    blocks = LEAVING[part]
    rows, units = hidden.shape

    def kernel(hidden_ref, down_ref, *refs):
        outs = refs[:-2]
        down_held, semaphores = refs[-2:]
        arriving = load_rows(Copies(semaphores), down_ref, down_held, blocks)
        for i in range(len(blocks)):
            wait(arriving[i])
            store_sum(part, i, dot(hidden_ref[...], down_held[i]).astype(BF), outs)

    return pl.pallas_call(
        kernel,
        in_specs=[VMEM, HBM],
        out_shape=sum_shapes(part, rows, width),
        scratch_shapes=row_buffers(blocks, width, units // 2) + semaphores_for(blocks, 1),
        compiler_params=LARGE,
        name=f"output_sums_{part}",
    )(hidden, down_flat)


def sum_shapes(part, rows, width):
    sizes = (HALF, HALF) if part == 0 else (rows,) * len(LEAVING[part])
    return [jax.ShapeDtypeStruct((size, width), BF) for size in sizes]


def store_sum(part, i, value, outs):
    if part == 0:
        outs[0][...] = value[:HALF]
        outs[1][...] = value[HALF:]
    else:
        outs[i][...] = value


def cotangents(part, pieces, down_flat, before=None, pre=None, weights=()):
    blocks = ARRIVING[part]
    rows, width = 2 * HALF, pieces[0].shape[1]
    hid = down_flat.shape[-2] // 2
    last = part == len(ARRIVING) - 1

    def kernel(*refs):
        count = len(pieces)
        held_pieces, refs = refs[:count], refs[count:]
        if before is not None:
            before_ref, refs = refs[0], refs[1:]
        if last:
            pre_ref, down_held, gate_held, up_held, *outs = refs
            arriving = [()]
        else:
            down_ref, *outs, down_held, semaphores = refs
            arriving = load_rows(Copies(semaphores), down_ref, down_held, blocks)
        first = row_slot((rows, hid))
        total = before_ref[...] if before is not None else None
        for i, value in enumerate(arrived_blocks(part, held_pieces)):
            wait(arriving[i])
            share = dot(value, down_held[i], NT)
            share = jnp.where(first, share[:, :hid], share[:, hid:])
            total = share if total is None else total + share
        if not last:
            outs[0][...] = total
            return
        gate, up = pre_ref[:, :hid], pre_ref[:, hid:]
        sigmoid = jax.nn.sigmoid(gate)
        gate_diff = (total * up * sigmoid * (1.0 + gate * (1.0 - sigmoid))).astype(BF)
        up_diff = (total * (gate * sigmoid)).astype(BF)
        gate_diff, up_diff = pair(first, gate_diff), pair(first, up_diff)
        outs[0][...] = gate_diff
        outs[1][...] = up_diff
        value = dot(gate_diff, both(gate_held, 0), NT) + dot(up_diff, both(up_held, 0), NT)
        store_sum(0, 0, value.astype(BF), outs[2:])

    if last:
        shapes = [jax.ShapeDtypeStruct((rows, 2 * hid), BF)] * 2 + sum_shapes(0, rows, width)
        scratch = []
    else:
        shapes = [jax.ShapeDtypeStruct((rows, hid), F32)]
        scratch = row_buffers(blocks, width, hid) + semaphores_for(blocks, 1)
    extra = [value for value in (before, pre) if value is not None]
    held = [VMEM if last else HBM] * (1 + len(weights))
    out = pl.pallas_call(
        kernel,
        in_specs=[VMEM] * (len(pieces) + len(extra)) + held,
        out_shape=shapes,
        scratch_shapes=scratch,
        compiler_params=LARGE,
        name=f"cotangents_{part}",
    )(*pieces, *extra, down_flat, *weights)
    return out if last else out[0]


def input_sums(part, diffs, weights, width):
    blocks = LEAVING[part]
    rows, units = diffs[0].shape

    def kernel(gate_diff_ref, up_diff_ref, gate_ref, up_ref, *refs):
        outs = refs[:-3]
        gate_held, up_held, semaphores = refs[-3:]
        arriving = load_columns(
            Copies(semaphores), (gate_ref, up_ref), (gate_held, up_held), blocks
        )
        for i in range(len(blocks)):
            wait(arriving[i])
            value = dot(gate_diff_ref[...], both(gate_held, i), NT)
            value += dot(up_diff_ref[...], both(up_held, i), NT)
            store_sum(part, i, value.astype(BF), outs)

    return pl.pallas_call(
        kernel,
        in_specs=[VMEM, VMEM, HBM, HBM],
        out_shape=sum_shapes(part, rows, width),
        scratch_shapes=column_buffers(blocks, width, units // 2) + semaphores_for(blocks, 2),
        compiler_params=LARGE,
        name=f"input_sums_{part}",
    )(*diffs, *weights)


def middle_sums(diffs, hidden, weights, down_flat, width):
    in_blocks, out_blocks = LEAVING[1:]
    rows, units = hidden.shape

    def kernel(gate_diff_ref, up_diff_ref, hidden_ref, gate_ref, up_ref, down_ref, *refs):
        outs = refs[:-4]
        gate_held, up_held, down_held, semaphores = refs[-4:]
        copies = Copies(semaphores)
        arriving = load_columns(copies, (gate_ref, up_ref), (gate_held, up_held), in_blocks)
        down_arriving = load_rows(copies, down_ref, down_held, out_blocks)
        for i in range(len(in_blocks)):
            wait(arriving[i])
            value = dot(gate_diff_ref[...], both(gate_held, i), NT)
            value += dot(up_diff_ref[...], both(up_held, i), NT)
            outs[i][...] = value.astype(BF)
        for i in range(len(out_blocks)):
            wait(down_arriving[i])
            outs[len(in_blocks) + i][...] = dot(hidden_ref[...], down_held[i]).astype(BF)

    out = pl.pallas_call(
        kernel,
        in_specs=[VMEM] * 3 + [HBM] * 3,
        out_shape=sum_shapes(1, rows, width) + sum_shapes(2, rows, width),
        scratch_shapes=column_buffers(in_blocks, width, units // 2)
        + row_buffers(out_blocks, width, units // 2)
        + semaphores_for(range(10), 1),
        compiler_params=LARGE,
        name="middle_sums",
    )(*diffs, hidden, *weights, down_flat)
    return out[: len(in_blocks)], out[len(in_blocks) :]


def all_blocks(pieces):
    at = 0
    for part, count in enumerate((4, 3, 2)):
        for block, value in zip(ARRIVING[part], arrived_blocks(part, pieces[at : at + count])):
            yield block, value
        at += count


def column_grads_kernel(*refs):
    pieces = refs[:9]
    diffs, outs, held, semaphores = refs[9:11], refs[11:13], refs[13:15], refs[15]
    width, hid = held[0].shape[2:]
    copies = Copies(semaphores)
    leaving = []
    for block, value in all_blocks(pieces):
        for diff_ref, out_ref, held_ref in zip(diffs, outs, held):
            grad = dot(value, diff_ref[...], TN).astype(BF)
            held_ref[block, 0] = grad[:, :hid]
            held_ref[block, 1] = grad[:, hid:]
            target = out_ref.at[:, features_of(block, width), :]
            leaving += copies.start([(held_ref.at[block], target)])
    wait(leaving)


def column_grads(pieces, diffs):
    width = pieces[0].shape[1]
    hid = diffs[0].shape[1] // 2
    blocks = range(8)
    return pl.pallas_call(
        column_grads_kernel,
        in_specs=[VMEM] * 11,
        out_specs=[HBM] * 2,
        out_shape=[jax.ShapeDtypeStruct((2, 8 * width, hid), BF)] * 2,
        scratch_shapes=column_buffers(blocks, width, hid) + semaphores_for(blocks, 2),
        compiler_params=LARGE,
        name="column_grads",
    )(*pieces, *diffs)


def row_grads_kernel(*refs):
    pieces = refs[:9]
    hidden_ref, down_out, held, semaphores = refs[9:]
    width = held.shape[2]
    copies = Copies(semaphores)
    leaving = []
    for block, value in all_blocks(pieces):
        held[block] = dot(hidden_ref[...], value, TN).astype(BF)
        target = down_out.at[:, features_of(block, width)]
        leaving += copies.start([(held.at[block], target)])
    wait(leaving)


def row_grads(pieces, hidden):
    width = pieces[0].shape[1]
    units = hidden.shape[1]
    blocks = range(8)
    return pl.pallas_call(
        row_grads_kernel,
        in_specs=[VMEM] * 10,
        out_specs=HBM,
        out_shape=jax.ShapeDtypeStruct((units, 8 * width), BF),
        scratch_shapes=row_buffers(blocks, width, units // 2) + semaphores_for(blocks, 1),
        compiler_params=LARGE,
        name="row_grads",
    )(*pieces, hidden)


def wide(value):
    return value.astype(F32)


def second_hop(low, far, above1, below1, got_up, got_down, to_up, to_down, to_side):
    high, cut = 2 * HALF - low, HALF - low
    to_up[:HALF] = far[:HALF]
    to_up[HALF:] = (wide(above1[:low]) + wide(got_up[:low])).astype(BF)
    to_down[:HALF] = far[HALF:]
    to_down[HALF:] = (wide(below1[high:]) + wide(got_down[cut:])).astype(BF)
    to_side[:cut] = (wide(above1[low:HALF]) + wide(got_up[low:])).astype(BF)
    to_side[cut:high] = above1[HALF:]
    to_side[high : high + HALF] = below1[:HALF]
    to_side[high + HALF :] = (wide(below1[HALF:high]) + wide(got_down[:cut])).astype(BF)


def third_hop(low, above, below, beside, got_up, got_down, got_side, to_up, to_down, to_side):
    high, cut = 2 * HALF - low, HALF - low
    to_up[:low] = (wide(above[:low]) + wide(got_up[:low])).astype(BF)
    to_up[low:HALF] = (
        wide(above[low:HALF]) + wide(got_up[low:HALF]) + wide(got_side[:cut])
    ).astype(BF)
    to_up[HALF:] = (wide(above[HALF:]) + wide(got_side[cut:high])).astype(BF)
    to_down[:HALF] = (wide(below[:HALF]) + wide(got_side[high : high + HALF])).astype(BF)
    to_down[HALF:high] = (
        wide(below[HALF:high]) + wide(got_side[high + HALF :]) + wide(got_down[:cut])
    ).astype(BF)
    to_down[high:] = (wide(below[high:]) + wide(got_down[cut:HALF])).astype(BF)
    to_side[:low] = (wide(beside[:low]) + wide(got_up[HALF:])).astype(BF)
    to_side[low:high] = beside[low:high]
    to_side[high:] = (wide(beside[high:]) + wide(got_down[HALF:])).astype(BF)


def out_second_kernel(*refs):
    second_hop(OUT_LOW, *refs)


def both_hops_kernel(*refs):
    size = 2 * HALF
    outs = refs[11:]
    third_hop(OUT_LOW, *refs[:6], *[ref.at[pl.ds(0, size)] for ref in outs])
    second_hop(IN_LOW, *refs[6:11], *[ref.at[pl.ds(size, ref.shape[0] - size)] for ref in outs])


def in_third_kernel(above, below, beside, got_up, got_down, got_side, *outs):
    size = 2 * HALF
    got = [ref.at[pl.ds(size, ref.shape[0] - size)] for ref in (got_up, got_down, got_side)]
    third_hop(IN_LOW, above, below, beside, *got, *outs)


def last_kernel(own, from_below, from_above, from_side, total):
    rows = slice(0, 2 * HALF)
    total[...] = (
        (wide(own[...]) + wide(from_side[rows]))
        + (wide(from_below[rows]) + wide(from_above[rows]))
    ).astype(BF)


def final_hop_kernel(above, below, beside, got_up, got_down, got_side, to_up, to_down, to_side):
    got = [ref.at[pl.ds(2 * HALF, ref.shape[0] - 2 * HALF)] for ref in (got_up, got_down, got_side)]
    third_hop_kernel(above, below, beside, *got, to_up, to_down, to_side)


class Sums:
    def __init__(self, links):
        self.links = links

    def send(self, to_up, to_down, to_side):
        links = self.links
        return (links.send_up(to_up), links.send_down(to_down), links.cross(to_side))

    def first(self, sums):
        return (self.links.send_up(sums[0]), self.links.send_down(sums[1]))

    def second(self, *args):
        outgoing = local_call(out_second_kernel, "second_hop", hop_sizes(OUT_LOW), *args)
        return outgoing, self.send(*outgoing)

    def both(self, *args):
        sizes = tuple(2 * HALF + size for size in hop_sizes(IN_LOW))
        outgoing = local_call(both_hops_kernel, "both_hops", sizes, *args)
        return outgoing, self.send(*outgoing)

    def last(self, *args):
        outgoing = local_call(in_third_kernel, "third_hop", (2 * HALF,) * 3, *args)
        return outgoing, self.send(*outgoing)

    def total(self, own, got):
        return local_call(last_kernel, "last_hop", (2 * HALF,), own, *got)[0]


def combine_kernel(pick_ref, gated_ref, rows_ref, mixed_ref, grads_ref):
    width = mixed_ref.shape[1]
    mixed_ref[...] = exact_dot(gated_ref[...], rows_ref[:, :width], TN).astype(BF)
    grads_ref[...] = dot(pick_ref[...], rows_ref[:, width:], TN).astype(BF)


def combine(pick, gated, rows):
    shape = jax.ShapeDtypeStruct((pick.shape[1], rows.shape[1] // 2), BF)
    return pl.pallas_call(
        combine_kernel, out_shape=[shape] * 2, compiler_params=SMALL, name="combine"
    )(pick, gated, rows)


def on_device(tokens, upstream, expert_ids, gate_values, gate_weight, up_weight, down_weight):
    columns = lax.axis_size("expert")
    exp_dev, hid, features = down_weight.shape
    rows = columns * exp_dev * 8
    width = tokens.shape[1]
    links = Links(lax.axis_size("dp"))
    columns_in = (in_hbm(gate_weight), in_hbm(up_weight))
    rows_in = in_hbm(down_weight.reshape(exp_dev * hid, features))

    def exchange(value):
        return lax.all_to_all(
            value.reshape(columns, exp_dev * 8, -1), "expert", 0, 0, tiled=True
        ).reshape(rows, -1)

    x_rows, c_rows, pick, gated = dispatch(expert_ids, gate_values, tokens, upstream, rows)
    arrived = exchange(jnp.concatenate([x_rows, c_rows], axis=1))
    x = Gather(links, arrived[:, :width])
    c = Gather(links, arrived[:, width:])
    x_sent = x.relay()
    pre = gate_up(0, after(x.arrived[0], *x_sent), columns_in)
    *last_columns, last_rows = fetch_last(after(columns_in, pre), rows_in, width)
    c_sent = c.relay(pre, last_rows)
    x_sent = x.ends(*c_sent)
    total = cotangents(0, after(c.arrived[0], *x_sent), rows_in)
    pre = gate_up(1, after(x.arrived[1], total), columns_in, pre)
    c_sent = c.ends(pre)
    total = cotangents(1, after(c.arrived[1], *c_sent), rows_in, total)
    pre, hidden, *out_cuts = gate_up(
        2, after(x.arrived[2], total), last_columns, pre, last_rows
    )

    hops = Sums(links)
    out_got = hops.first(out_cuts)
    out_far = output_sums(1, after(hidden, *out_cuts), rows_in, width)
    *diffs, cut_up, cut_down = cotangents(
        2, after(c.arrived[2], *out_far), last_rows, total, pre, last_columns
    )
    in_got = hops.first((cut_up, cut_down))
    sent, out_got = hops.second(*out_far, *after(out_got, cut_up))
    in_far, out_near = middle_sums(after(diffs, *sent), hidden, columns_in, rows_in, width)
    sent, got = hops.both(*out_near[:3], *out_got, *in_far, *in_got)
    in_near = input_sums(2, after(diffs, *sent), columns_in, width)
    down_grad = row_grads(after(sum(c.arrived, ()), *in_near), hidden)
    gate_grad, up_grad = column_grads(after(sum(x.arrived, ()), down_grad), diffs)
    sent, in_got = hops.last(*in_near[:3], *after(got, gate_grad))
    out_total = hops.total(out_near[3], after(got, *sent))
    in_total = hops.total(in_near[3], after(in_got, out_total))
    returned = exchange(jnp.concatenate([out_total, in_total], axis=1))
    mixed, token_grads = combine(pick, gated, returned)
    return (mixed, token_grads, gate_grad, up_grad, down_grad.reshape(down_weight.shape))


def solution(mesh):
    return jax.shard_map(
        on_device,
        mesh=mesh,
        in_specs=(
            P("expert", "dp"),
            P("expert", "dp"),
            P("expert", None),
            P("expert", None),
            P("expert", None, "dp"),
            P("expert", None, "dp"),
            P("expert", "dp", None),
        ),
        out_specs=(
            P("expert", "dp"),
            P("expert", "dp"),
            P("expert", None, "dp"),
            P("expert", None, "dp"),
            P("expert", "dp", None),
        ),
        check_vma=False,
    )
```
